32 devices in a mesh: group: 2 (over y), ep: 4 (over z), pd: 4 (over x, core).
Axes of the slice: x: 2, y: 2, z: 4, core: 2. Of those that a mesh axis runs over, the one named last changes fastest.
Arguments:
- tokens: bfloat16 [2048, 7168], P(('group', 'ep'), 'pd'), parts along dimension 0, may hold values from -6 to 6
- expert_ids: int32 [2048, 8], P(('group', 'ep')), parts along dimension 0, may hold values from 0 to 255, all different within a row; in each aligned block of 256 rows (0 to 255, 256 to 511, ...) at most 16 rows name the same one
- gate_scores: float32 [2048, 8], P(('group', 'ep')), parts along dimension 0, may hold values from 0.1 to 1
- gate_weight: bfloat16 [4, 7168, 1024], P('ep', None, 'pd'), may hold values from -0.0625 to 0.0625
- up_weight: bfloat16 [4, 7168, 1024], P('ep', None, 'pd'), may hold values from -0.0625 to 0.0625
- down_weight: bfloat16 [4, 1024, 7168], P('ep', 'pd'), may hold values from -0.1875 to 0.1875
- cache_rows: bfloat16 [32, 32, 576], P(('group', 'ep'), 'pd'), parts along dimension 0, may hold values from -6 to 6
- lengths: int32 [32], P('group'), parts along dimension 0, may hold values from 1 to 32, 256 in all
- destination: int32 [8, 4], P('group'), parts along dimension 0, may hold values from 0 to 3, as said below
- decode_query: bfloat16 [8, 4, 64, 576], P(('group', 'ep'), None, 'pd'), parts along dimension 0, may hold values from -450 to 450
Outputs:
- mixed: bfloat16 [2048, 7168], P(('group', 'ep'), 'pd'), parts along dimension 0
- attended: bfloat16 [8, 4, 64, 512], P(('group', 'ep'), None, 'pd'), parts along dimension 0
The draws below stay inside these ranges and needn't reach their ends.
There are 2 independent parts, one for each index of `group`. The reference program is written for one: setup_inputs(seed, part) draws one part's arguments, and reference() takes and returns one part's arrays. A program takes and returns all parts, laid end to end along the dimension named above; an argument that names none is the same for every part. Nothing has to cross between parts.
Inputs may be any that keep to these rules, and one draw needn't show every extreme that they name: `expert_ids`: each row names 8 different experts; within each aligned block of 256 rows, the rows of one ep index, no expert is named by more than 16 rows. `destination`: each row is a permutation: every decode index receives exactly one request from each ep index.
All inputs are finite; a program needn't handle non-finite values.
Results may differ from the reference program's by a relative error of at most 0.012.
Values may be sent and summed in bfloat16 or wider, within the bound.
No kernel may reach another device: no remote copies, remote signals or barrier semaphores. Data moves between devices by JAX's collectives and lax.ppermute only.
A program may use at most 128 MiB of HBM per device.

```python
import math
import jax
import jax.numpy as jnp
import numpy as np
from jax import lax

D = 7168
NEXP = 256
TOPK = 8
LATC = 512
FFW = 1024
HEADS = 64
TOK_DEV = 256
CTX = 32
LATR = 576
CAP = 16
NWIN = 4
TOKENS = 1024
REQS = 16
N_EP = 4


def shared_draw(key):
    row_keys = jax.random.split(jax.random.fold_in(key, 101), N_EP)
    routes = jax.vmap(lambda sub_key: jax.random.permutation(sub_key, N_EP))(row_keys).astype(jnp.int32)
    base = jax.random.normal(jax.random.fold_in(key, 202), (REQS, CTX, LATR), jnp.float32)
    second = base[:, 1, LATC:]
    base = base.at[:, 1, LATC:].set(second)
    return (routes, jnp.clip(base, -6.0, 6.0))


def draw_destination(key, part):
    routes, unused_rows = shared_draw(key)
    return routes


def draw_cache_rows(key, part):
    routes, base = shared_draw(key)
    return base.astype(jnp.bfloat16)


def draw_decode_query(key, part):
    key = jax.random.fold_in(key, 3)
    queries = 0.5 * jax.random.normal(jax.random.fold_in(key, 1), (N_EP, N_EP, HEADS, LATR), jnp.float32)
    return queries.astype(jnp.bfloat16)


def level_of(key, dims, cuts, low, high):
    loudness = 1.0
    for position, blocks in cuts:
        steps = jax.random.uniform(jax.random.fold_in(jax.random.fold_in(key, 6), position), (blocks,), jnp.float32, low / len(cuts), high / len(cuts))
        loudness = loudness * jnp.repeat(jnp.exp(steps), dims[position] // blocks).reshape((-1,) + (1,) * (len(dims) - 1 - position))
    return loudness


def split_up(amount, total, limit, slope):
    weights = [(1 << 20) // math.isqrt(standing ** slope) + 1 for standing in range(2, amount + 1)]
    spare, holding = total - limit - (amount - 1), [1] * (amount - 1)
    while spare > 0:
        movable = [i for i in range(amount - 1) if holding[i] < limit]
        pool, remaining = sum([weights[i] for i in movable]), spare
        for i in movable:
            addition = min(limit - holding[i], max(1, remaining * weights[i] // pool), spare)
            holding[i] = holding[i] + addition
            spare = spare - addition
    return np.array([limit] + holding)


def uneven(own_key, count, total, reach, slope):
    if count == 2:
        one = jax.random.randint(own_key, (), max(1, total - reach), min(reach, total - 1) + 1)
        return jnp.stack([one, total - one])
    sizes = jnp.asarray(split_up(count, total, reach, slope), jnp.int32)
    couples = (count - 1) // 2
    source_of, receiver = sizes[1:1 + 2 * couples:2], sizes[2:2 + 2 * couples:2]
    slack = jnp.minimum(source_of - 1, reach - receiver)
    moved = jax.random.randint(jax.random.fold_in(own_key, 1), (couples,), 0, 1 << 20) % (slack + 1)
    sizes = sizes.at[1:1 + 2 * couples:2].set(source_of - moved).at[2:2 + 2 * couples:2].set(receiver + moved)
    return sizes[jax.random.permutation(jax.random.fold_in(own_key, 2), count)]


def deal_out(stream_key, own, number, rows, amount, top, bound, slope):
    ranking = jax.random.permutation(stream_key, amount)
    crowded, usual = portions_of(amount, rows * top, bound, slope, True), portions_of(amount, rows * top, bound, slope, False)
    places = jnp.arange(amount)

    def named(sizes, rotation):
        used = int((sizes > 0).sum())
        fixed = max(1, used // 4)
        passed = fixed + (places - fixed + rotation * (used - fixed)) % max(1, amount - fixed)
        return jnp.zeros((amount,), jnp.int32).at[ranking[jnp.where(places < fixed, places, passed)]].set(jnp.asarray(sizes, jnp.int32))

    sizes = jnp.where(number % 4 == 0, named(crowded, number // 4), named(usual, number - number // 4 - 1))
    mixed = jax.random.permutation(jax.random.fold_in(own, 3), amount)
    source_of, taker = mixed[0:amount // 2 * 2:2], mixed[1:amount // 2 * 2:2]
    slack = jnp.minimum(sizes[source_of] - 1, bound - sizes[taker]) // 2
    slack = jnp.where((source_of == ranking[0]) | (taker == ranking[0]) | (sizes[taker] == 0), 0, jnp.maximum(slack, 0))
    passed = jax.random.randint(jax.random.fold_in(own, 4), (amount // 2,), 0, 1 << 20) % (slack + 1)
    sizes = sizes.at[source_of].add(-passed).at[taker].add(passed)
    labels = jnp.searchsorted(jnp.cumsum(sizes), jnp.arange(rows * top), side="right").astype(jnp.int32)
    listing = labels.reshape(top, rows).T
    listing = listing[jax.random.permutation(jax.random.fold_in(own, 1), rows)]
    rotation = jax.random.randint(jax.random.fold_in(own, 2), (rows, 1), 0, top)
    return jnp.take_along_axis(listing, (jnp.arange(top)[None, :] + rotation) % top, axis=1)


def portions_of(count, total, most, lean, full):
    loads = [(1 << 20) // math.isqrt(standing ** lean) + 1 for standing in range(1, count + 1)]
    largest = most if full else min(most, max(-(-total // count), total * loads[0] // sum(loads)))
    least = 1 if total - largest >= count - 1 else 0
    given, spare = [largest] + [least] * (count - 1), total - largest - least * (count - 1)
    while spare > 0:
        free = [i for i in range(1, count) if given[i] < largest] or [i for i in range(1, count) if given[i] < most]
        pool, left = sum([loads[i] for i in free]), spare
        for i in free:
            extra = min(most - given[i], max(1, left * loads[i] // pool), spare)
            given[i] = given[i] + extra
            spare = spare - extra
    return np.array(given)


def normal_values(key, shape, width, reach, cuts=(), held_as=jnp.bfloat16):
    result = width * jax.random.normal(key, shape, jnp.float32)
    if cuts:
        result = result * level_of(key, shape, cuts, -0.22, 0.18)
    return jnp.clip(result, -reach, reach).astype(held_as)


def setup_inputs(seed: int = 0, part: int = 0) -> dict:
    key_of = jax.random.split(jax.random.key(seed), 11)
    part_splits = jax.random.split(jax.random.fold_in(key_of[10], part), 11)
    tokens = normal_values(part_splits[0], (TOKENS, D), 1.0, 6.0, ((0, 4), (1, 4)))
    expert_ids_keys = jax.random.split(jax.random.fold_in(part_splits[1], 1), TOKENS // TOK_DEV)
    expert_ids_turns = jax.random.permutation(jax.random.fold_in(part_splits[1], 3), TOKENS // TOK_DEV)
    expert_ids = jax.vmap(lambda own, number: deal_out(jax.random.fold_in(part_splits[1], 2), own, number, TOK_DEV, NEXP, TOPK, CAP, 2))(expert_ids_keys, expert_ids_turns).reshape((TOKENS, TOPK))
    gate_scores = jnp.clip(0.1 + 0.9 * jax.random.uniform(part_splits[2], (TOKENS, TOPK), jnp.float32) ** level_of(part_splits[2], (TOKENS, TOPK), ((0, 4),), -0.2, 0.2), 0.1, 1.0)
    gate_weight = normal_values(key_of[3], (NWIN, D, FFW), D ** -0.5, 0.0625, ((0, 4), (2, 4)))
    up_weight = normal_values(key_of[4], (NWIN, D, FFW), D ** -0.5, 0.0625, ((0, 4), (2, 4)))
    down_weight = normal_values(key_of[5], (NWIN, FFW, D), FFW ** -0.5, 0.1875, ((0, 4), (1, 4)))
    cache_rows = draw_cache_rows(jax.random.fold_in(jax.random.fold_in(key_of[10], part), 71), part)
    lengths = uneven(part_splits[7], REQS, REQS * CTX // 2, CTX, 2).astype(jnp.int32)
    destination = draw_destination(jax.random.fold_in(jax.random.fold_in(key_of[10], part), 71), part)
    decode_query = draw_decode_query(jax.random.fold_in(jax.random.fold_in(key_of[10], part), 71), part)
    return {"tokens": tokens, "expert_ids": expert_ids, "gate_scores": gate_scores, "gate_weight": gate_weight, "up_weight": up_weight, "down_weight": down_weight, "cache_rows": cache_rows, "lengths": lengths, "destination": destination, "decode_query": decode_query}


score_scale = 192.0 ** -0.5


def window_targets(block_ids):
    flat_ids = block_ids.reshape(-1)
    in_window = flat_ids < N_EP
    matches = (flat_ids[:, None] == jnp.arange(N_EP, dtype=jnp.int32)[None, :]) & in_window[:, None]
    earlier = jnp.cumsum(matches.astype(jnp.int32), axis=0) - 1
    within = jnp.sum(jnp.where(matches, earlier, 0), axis=1)
    return jnp.where(in_window, flat_ids * CAP + within, N_EP * CAP).astype(jnp.int32)


def reference(tokens, expert_ids, gate_scores, gate_weight, up_weight, down_weight, cache_rows, lengths, destination, decode_query):
    targets = jax.vmap(window_targets)(expert_ids.reshape(N_EP, TOK_DEV * TOPK))
    owner_token = jnp.repeat(jnp.arange(TOK_DEV, dtype=jnp.int32), TOPK)
    source_base = (jnp.arange(N_EP, dtype=jnp.int32) * TOK_DEV)[:, None]
    slot_table = jnp.full((N_EP, N_EP * CAP + 1), -1, jnp.int32)
    slot_table = slot_table.at[jnp.arange(N_EP, dtype=jnp.int32)[:, None], targets].set(owner_token[None, :] + source_base)
    slot_table = slot_table[:, : N_EP * CAP].reshape(N_EP, N_EP, CAP)

    def expert_apply(expert_index):
        picks = lax.dynamic_index_in_dim(slot_table, expert_index, 1, keepdims=False).reshape(-1)
        expert_rows = jnp.where((picks >= 0)[:, None], tokens[jnp.maximum(picks, 0)], jnp.zeros((), tokens.dtype))
        w_gate = lax.dynamic_index_in_dim(gate_weight, expert_index, 0, keepdims=False)
        w_up = lax.dynamic_index_in_dim(up_weight, expert_index, 0, keepdims=False)
        w_down = lax.dynamic_index_in_dim(down_weight, expert_index, 0, keepdims=False)
        gate_sums = jnp.dot(expert_rows, w_gate, preferred_element_type=jnp.float32)
        up_sums = jnp.dot(expert_rows, w_up, preferred_element_type=jnp.float32)
        hidden = (jax.nn.silu(gate_sums) * up_sums).astype(jnp.bfloat16)
        return jnp.dot(hidden, w_down, preferred_element_type=jnp.float32).astype(jnp.bfloat16)

    expert_out = lax.map(expert_apply, jnp.arange(N_EP, dtype=jnp.int32))
    by_source = expert_out.reshape(N_EP, N_EP, CAP, D).transpose(1, 0, 2, 3).reshape(N_EP, N_EP * CAP, D)

    def combine_source(operands):
        source_out, source_targets, source_gates = operands
        padded = jnp.concatenate([source_out, jnp.zeros((1, D), source_out.dtype)], axis=0)
        picked = padded[source_targets].astype(jnp.float32).reshape(TOK_DEV, TOPK, D)
        return jnp.sum(picked * source_gates[:, :, None], axis=1).astype(jnp.bfloat16)

    mixed = lax.map(combine_source, (by_source, targets, gate_scores.reshape(N_EP, TOK_DEV, TOPK))).reshape(TOKENS, D)

    ep_range = jnp.arange(N_EP, dtype=jnp.int32)
    own_k = jnp.sum(jnp.where(destination[:, :, None] == ep_range[None, None, :], ep_range[None, :, None], 0), axis=1)
    request_index = (ep_range[:, None] * N_EP + own_k).T.astype(jnp.int32)
    key_rows = cache_rows[request_index].astype(jnp.float32)
    slot_lengths = lengths[request_index]
    scores = jnp.einsum("djhc,djtc->djht", decode_query.astype(jnp.float32), key_rows) * score_scale
    usable = jnp.arange(CTX, dtype=jnp.int32)[None, None, None, :] < slot_lengths[:, :, None, None]
    row_max = jnp.max(jnp.where(usable, scores, -1e30), axis=3, keepdims=True)
    weights_f32 = jnp.where(usable, jnp.exp(scores - row_max), 0.0)
    weights_bf16 = lax.optimization_barrier(weights_f32.astype(jnp.bfloat16)).astype(jnp.float32)
    weighted = jnp.einsum("djht,djtc->djhc", weights_bf16, key_rows[..., :LATC])
    attended = (weighted / jnp.sum(weights_f32, axis=3)[..., None]).astype(jnp.bfloat16)
    return (mixed, attended)
```

```python
import jax
import jax.numpy as jnp
from jax import lax
from jax.sharding import PartitionSpec as P

LATC = 512
CAP = 16

score_scale = 192.0 ** (-0.5)


def swap(value, axis, mask):
    count = lax.axis_size(axis)
    return lax.ppermute(value, axis, [(i, i ^ mask) for i in range(count)])


def on_device(
    tokens,
    expert_ids,
    gate_scores,
    gate_weight,
    up_weight,
    down_weight,
    cache_rows,
    lengths,
    destination,
    decode_query,
):
    ep_count = lax.axis_size("ep")
    own = lax.axis_index("ep")
    pd_count = lax.axis_size("pd")
    me = lax.axis_index("pd")
    token_count, width = tokens.shape
    bf16, f32 = jnp.bfloat16, jnp.float32
    partners = own ^ jnp.arange(ep_count, dtype=jnp.int32)

    ids = expert_ids.T
    gates = gate_scores.T
    named = ids[None] == partners[:, None, None]
    served = jnp.any(named, axis=1)
    gate = jnp.sum(jnp.where(named, gates[None], 0.0), axis=1)
    steps = jnp.arange(token_count, dtype=jnp.int32)
    earlier = (steps[:, None] < steps[None, :]).astype(bf16)
    rank = jnp.dot(served.astype(bf16), earlier, preferred_element_type=f32).astype(jnp.int32)
    slots = jnp.arange(CAP, dtype=jnp.int32)
    chosen = served[:, None, :] & (rank[:, None, :] == slots[None, :, None])
    dispatch = chosen.astype(bf16).reshape(ep_count * CAP, token_count)
    combine = jnp.where(chosen, gate[:, None, :], 0.0).reshape(ep_count * CAP, token_count)

    payload = jnp.dot(dispatch, tokens, preferred_element_type=f32).astype(bf16)
    payload = payload.reshape(ep_count, CAP, width)

    routes = lax.dynamic_index_in_dim(destination, own, 0, keepdims=False)
    pick = (routes[None, :] == partners[:, None]).astype(bf16)
    outgoing = jnp.einsum("dk,kpc->dpc", pick, cache_rows, preferred_element_type=f32).astype(bf16)

    rows = [payload[0]] + [swap(payload[d], "ep", d) for d in range(1, ep_count)]
    kept = [outgoing[0]] + [swap(outgoing[d], "ep", d) for d in range(1, ep_count)]
    rows = jnp.concatenate(rows, axis=0)
    kept = jnp.stack(kept, axis=0)

    pieces, caches = {0: rows}, {0: kept}
    bit = pd_count // 2
    while bit:
        for m in list(pieces):
            pieces[m ^ bit] = swap(pieces[m], "pd", bit)
            caches[m ^ bit] = swap(caches[m], "pd", bit)
        bit //= 2

    w_gate, w_up, w_down = gate_weight[0], up_weight[0], down_weight[0]
    gate_sums = up_sums = 0.0
    for m in sorted(pieces):
        start = (me ^ m) * width
        gate_sums += jnp.dot(
            pieces[m],
            lax.dynamic_slice_in_dim(w_gate, start, width, 0),
            preferred_element_type=f32,
        )
        up_sums += jnp.dot(
            pieces[m], lax.dynamic_slice_in_dim(w_up, start, width, 0), preferred_element_type=f32
        )
    hidden = (jax.nn.silu(gate_sums) * up_sums).astype(bf16)
    parts = {}
    for m in sorted(pieces):
        start = (me ^ m) * width
        parts[m] = jnp.dot(
            hidden,
            lax.dynamic_slice_in_dim(w_down, start, width, 1),
            preferred_element_type=f32,
        ).astype(bf16)
    bit = 1
    while bit < pd_count:
        for m in list(parts):
            if m & bit:
                arrived = swap(parts.pop(m), "pd", bit)
                kept_part = parts[m ^ bit].astype(f32) + arrived.astype(f32)
                parts[m ^ bit] = kept_part.astype(bf16)
        bit *= 2
    expert_out = parts[0].reshape(ep_count, CAP, width)
    returned = [expert_out[0]] + [swap(expert_out[d], "ep", d) for d in range(1, ep_count)]
    returned = jnp.concatenate(returned, axis=0)
    high = combine.astype(bf16)
    low = (combine - high.astype(f32)).astype(bf16)
    mixed = jnp.einsum("st,sd->td", high, returned, preferred_element_type=f32)
    mixed += jnp.einsum("st,sd->td", low, returned, preferred_element_type=f32)
    mixed = mixed.astype(bf16)

    order = partners
    queries = decode_query[0][order]
    keys = jnp.concatenate([caches[m] for m in sorted(caches)], axis=1)
    part_rows = cache_rows.shape[1]
    positions = jnp.concatenate(
        [(me ^ m) * part_rows + jnp.arange(part_rows, dtype=jnp.int32) for m in sorted(caches)]
    )
    slot_lengths = jnp.sum(
        jnp.where(destination == own, lengths.reshape(ep_count, ep_count), 0), axis=1
    )[order]
    scores = jnp.einsum("jhc,jtc->jht", queries, keys, preferred_element_type=f32) * score_scale
    usable = (positions[None, :] < slot_lengths[:, None])[:, None, :]
    top = jnp.max(jnp.where(usable, scores, -1e30), axis=2, keepdims=True)
    weights = jnp.where(usable, jnp.exp(scores - top), 0.0)
    total = jnp.sum(weights, axis=2, keepdims=True)
    summed = jnp.einsum(
        "jht,jtc->jhc", weights.astype(bf16), keys[:, :, :LATC], preferred_element_type=f32
    )
    attended = (summed / total).astype(bf16)[order][None]
    return (mixed, attended)


def solution(mesh):
    in_specs = (
        P(("group", "ep"), "pd"),
        P(("group", "ep"), None),
        P(("group", "ep"), None),
        P("ep", None, "pd"),
        P("ep", None, "pd"),
        P("ep", "pd", None),
        P(("group", "ep"), "pd", None),
        P("group"),
        P("group", None),
        P(("group", "ep"), None, "pd", None),
    )
    out_specs = (P(("group", "ep"), "pd"), P(("group", "ep"), None, "pd", None))
    return jax.shard_map(
        on_device, mesh=mesh, in_specs=in_specs, out_specs=out_specs, check_vma=False
    )
```

```python
import functools

import jax
import jax.numpy as jnp
from jax import lax
from jax.experimental import pallas as pl
from jax.experimental.pallas import tpu as pltpu
from jax.sharding import PartitionSpec as P

LATC = 512
CAP = 16

score_scale = 192.0 ** (-0.5)

bf16, f32, i32 = jnp.bfloat16, jnp.float32, jnp.int32
VMEM = pl.BlockSpec(memory_space=pltpu.VMEM)
SMEM = pl.BlockSpec(memory_space=pltpu.SMEM)
HBM = pl.BlockSpec(memory_space=pltpu.HBM)
ANY = pl.BlockSpec(memory_space=pl.ANY)


def swap(value, axis, mask):
    count = lax.axis_size(axis)
    return lax.ppermute(value, axis, [(i, i ^ mask) for i in range(count)])


def in_hbm(value):
    return pltpu.with_memory_space_constraint(value, pltpu.HBM)


def params(arrays, extra=6 << 20):
    held = sum(a.size * a.dtype.itemsize for a in arrays)
    return pltpu.CompilerParams(vmem_limit_bytes=min(held + extra, 60 << 20))


def cost(flops, moved=0):
    return pl.CostEstimate(flops=flops, bytes_accessed=moved, transcendentals=0)


def fold_widths(latr):
    first = latr // 2 // 128 * 128
    return first, latr - first, -(-(latr - first) // 128) * 128


def route_kernel(ep_count, ids_ref, gates_ref, tokens_ref, cache_ref, dest_ref, *outs):
    blocks, combine_ref = outs[:-1], outs[-1]
    own = lax.axis_index("ep")
    token_count, width = tokens_ref.shape
    ids, gates = ids_ref[...], gates_ref[...]
    served, gate = [], []
    for d in range(ep_count):
        named = ids == (own ^ d)
        served.append(jnp.sum(jnp.where(named, 1.0, 0.0), axis=0, keepdims=True))
        gate.append(jnp.sum(jnp.where(named, gates, 0.0), axis=0, keepdims=True))
    shape = (token_count, token_count)
    before = lax.broadcasted_iota(i32, shape, 0) < lax.broadcasted_iota(i32, shape, 1)
    before = jnp.where(before, 1.0, 0.0).astype(bf16)
    marks = jnp.concatenate(served, axis=0)
    rank = jnp.dot(marks.astype(bf16), before, preferred_element_type=f32)
    rank = jnp.where(marks > 0.5, rank, -1.0)
    slots = lax.broadcasted_iota(i32, (CAP, token_count), 0).astype(f32)
    chosen = [slots == rank[d : d + 1] for d in range(ep_count)]
    dispatch = jnp.concatenate([jnp.where(c, 1.0, 0.0) for c in chosen], axis=0).astype(bf16)
    rows = jnp.dot(dispatch, tokens_ref[...], preferred_element_type=f32)
    first, second, wide = fold_widths(cache_ref.shape[2])
    part = cache_ref.shape[1]
    for d in range(ep_count):
        combine_ref[d * CAP : (d + 1) * CAP, :] = jnp.where(chosen[d], gate[d], 0.0)
        blocks[d][:, :width] = rows[d * CAP : (d + 1) * CAP].astype(bf16)
        pick = i32(0)
        for k in range(ep_count):
            pick = jnp.where(dest_ref[own, k] == (own ^ d), k, pick)
        kept = cache_ref[pick].astype(f32)
        above = jnp.concatenate([kept[:, :first], jnp.zeros((part, wide - first), f32)], axis=1)
        below = jnp.concatenate([kept[:, first:], jnp.zeros((part, wide - second), f32)], axis=1)
        blocks[d][:, width:] = jnp.concatenate([above, below], axis=0).astype(bf16)


def route(ids, gates, tokens, cache_rows, destination, ep_count):
    token_count, width = tokens.shape
    wide = fold_widths(cache_rows.shape[2])[2]
    out_shape = [jax.ShapeDtypeStruct((CAP, width + wide), bf16)] * ep_count
    out_shape += [jax.ShapeDtypeStruct((ep_count * CAP, token_count), f32)]
    outs = pl.pallas_call(
        functools.partial(route_kernel, ep_count),
        out_shape=out_shape,
        in_specs=[VMEM, VMEM, VMEM, VMEM, SMEM],
        out_specs=[VMEM] * (ep_count + 1),
        compiler_params=params([tokens, ids, gates, cache_rows] + out_shape * 2),
        cost_estimate=cost(4 * ep_count * CAP * tokens.size, 2 * tokens.size),
        name="route",
    )(*map(in_hbm, (ids, gates, tokens, cache_rows, destination)))
    return outs[:-1], outs[-1]


def fetch_kernel(cuts, after_ref, *refs):
    count = (len(refs) - 2) // 2
    sems, mark_ref = refs[-1], refs[-2]
    copies = []
    for i in range(count):
        rows = refs[i].shape[0] // cuts
        for c in range(cuts):
            at = pl.ds(c * rows, rows)
            copies.append(
                pltpu.make_async_copy(refs[i].at[at], refs[count + i].at[at], sems.at[i, c])
            )
    for copy in copies:
        copy.start()
    mark_ref[...] = jnp.zeros(mark_ref.shape, mark_ref.dtype)
    for copy in copies:
        copy.wait()


def fetch(after, *arrays):
    out_shape = [pltpu.VMEM(a.shape, a.dtype) for a in arrays]
    cuts = 4
    outs = pl.pallas_call(
        functools.partial(fetch_kernel, cuts),
        out_shape=out_shape + [jax.ShapeDtypeStruct((8, 128), f32)],
        in_specs=[ANY] + [HBM] * len(arrays),
        out_specs=[VMEM] * (len(arrays) + 1),
        scratch_shapes=[pltpu.SemaphoreType.DMA((len(arrays), cuts))],
        compiler_params=pltpu.CompilerParams(vmem_limit_bytes=1 << 20),
        cost_estimate=cost(0, 0),
        name="fetch",
    )(after, *map(in_hbm, arrays))
    return outs[:-1], outs[-1]


def join_kernel(count, *refs):
    out_ref, at = refs[-1], 0
    for ref in refs[:count]:
        out_ref[at : at + ref.shape[0], :] = ref[...]
        at += ref.shape[0]


def join(blocks, after=(), weight=0):
    rows = sum(b.shape[0] for b in blocks)
    out_shape = jax.ShapeDtypeStruct((rows, blocks[0].shape[1]), blocks[0].dtype)
    return pl.pallas_call(
        functools.partial(join_kernel, len(blocks)),
        out_shape=out_shape,
        in_specs=[VMEM] * len(blocks) + [ANY] * len(after),
        out_specs=VMEM,
        compiler_params=params([out_shape] * 3, 1 << 20),
        cost_estimate=cost(0, weight),
        name="join",
    )(*blocks, *after)


def tie_kernel(*refs):
    pass


def tie(value, after):
    return pl.pallas_call(
        tie_kernel,
        out_shape=jax.ShapeDtypeStruct(value.shape, value.dtype),
        in_specs=[ANY] * (1 + len(after)),
        out_specs=ANY,
        input_output_aliases={0: 0},
        compiler_params=pltpu.CompilerParams(vmem_limit_bytes=1 << 20),
        cost_estimate=cost(0, 0),
        name="tie",
    )(value, *after)


def total_kernel(kept_ref, arrived_ref, *outs):
    at = 0
    for out in outs:
        rows = pl.ds(at, out.shape[0])
        out[...] = (kept_ref[rows, :] + arrived_ref[rows, :].astype(f32)).astype(out.dtype)
        at += out.shape[0]


def total(kept, arrived, count, dtype=bf16):
    rows, columns = kept.shape
    out_shape = [jax.ShapeDtypeStruct((rows // count, columns), dtype)] * count
    return pl.pallas_call(
        total_kernel,
        out_shape=out_shape,
        in_specs=[VMEM, VMEM],
        out_specs=[VMEM] * count,
        compiler_params=params([kept] * 4, 1 << 20),
        cost_estimate=cost(kept.size, 8 * kept.size),
        name="total",
    )(kept, arrived)


def piece_sums(piece_refs, masks, me, width, gate_ref, up_ref):
    gate_sums = up_sums = None
    for refs, m in zip(piece_refs, masks):
        rows = jnp.concatenate([r[:, :width] for r in refs], axis=0)
        at = pl.ds(pl.multiple_of((me ^ m) * width, width), width)
        g = jnp.dot(rows, gate_ref[at, :], preferred_element_type=f32)
        u = jnp.dot(rows, up_ref[at, :], preferred_element_type=f32)
        gate_sums = g if gate_sums is None else gate_sums + g
        up_sums = u if up_sums is None else up_sums + u
    return gate_sums, up_sums


def first_kernel(masks, width, gate_ref, up_ref, *refs):
    pieces, (gate_out, up_out) = refs[:-2], refs[-2:]
    per = len(pieces) // len(masks)
    groups = [pieces[i * per : (i + 1) * per] for i in range(len(masks))]
    gate_out[...], up_out[...] = piece_sums(
        groups, masks, lax.axis_index("pd"), width, gate_ref, up_ref
    )


def second_kernel(
    masks, targets, width, gate_ref, up_ref, down_ref, gsum_ref, usum_ref, *refs
):
    outs = refs[len(refs) - len(targets) - 1 :]
    pieces, hidden_out = refs[: len(refs) - len(targets) - 1], outs[-1]
    per = len(pieces) // len(masks)
    groups = [pieces[i * per : (i + 1) * per] for i in range(len(masks))]
    me = lax.axis_index("pd")
    gate_sums, up_sums = piece_sums(groups, masks, me, width, gate_ref, up_ref)
    gate_sums, up_sums = gate_sums + gsum_ref[...], up_sums + usum_ref[...]
    hidden = (gate_sums / (1.0 + jnp.exp(-gate_sums)) * up_sums).astype(bf16)
    hidden_out[...] = hidden
    for out, m in zip(outs, targets):
        at = pl.ds(pl.multiple_of((me ^ m) * width, width), width)
        out[...] = jnp.dot(hidden, down_ref[:, at], preferred_element_type=f32).astype(bf16)


def third_kernel(targets, width, hidden_ref, down_ref, *outs):
    me = lax.axis_index("pd")
    for out, m in zip(outs, targets):
        at = pl.ds(pl.multiple_of((me ^ m) * width, width), width)
        out[...] = jnp.dot(hidden_ref[...], down_ref[:, at], preferred_element_type=f32)


def attend_kernel(
    ep_count, pd_count, width, dest_ref, len_ref, query_ref, *refs
):
    pieces, out_ref = refs[:-1], refs[-1]
    per = len(pieces) // pd_count
    own, me = lax.axis_index("ep"), lax.axis_index("pd")
    latr, heads = query_ref.shape[2], query_ref.shape[1]
    first, second, wide = fold_widths(latr)
    part = CAP // 2
    shape = (heads, part * pd_count)
    column = lax.broadcasted_iota(i32, shape, 1)
    position = (me ^ (column // part)) * part + column % part
    sizes = [pieces[g].shape[0] // CAP for g in range(per)]
    where = [(g, i) for g in range(per) for i in range(sizes[g])]
    for d in range(ep_count):
        j = own ^ d
        length = i32(0)
        for k in range(ep_count):
            length = jnp.where(dest_ref[j, k] == own, len_ref[j * ep_count + k], length)
        keys = []
        for m in range(pd_count):
            ref = pieces[m * per + where[d][0]]
            at = where[d][1] * CAP
            folded = ref[at : at + CAP, width:].astype(f32)
            keys.append(
                jnp.concatenate([folded[:part, :first], folded[part:, :second]], axis=1)
            )
        keys = jnp.concatenate(keys, axis=0).astype(bf16)
        scores = lax.dot_general(
            query_ref[j], keys, (((1,), (1,)), ((), ())), preferred_element_type=f32
        )
        scores = scores * score_scale
        usable = position < length
        top = jnp.max(jnp.where(usable, scores, -1e30), axis=1, keepdims=True)
        weights = jnp.where(usable, jnp.exp(scores - top), 0.0)
        total = jnp.sum(weights, axis=1, keepdims=True)
        summed = jnp.dot(weights.astype(bf16), keys[:, :LATC], preferred_element_type=f32)
        out_ref[j] = (summed / total).astype(bf16)


def combine_kernel(combine_ref, *refs):
    blocks, out_ref = refs[:-1], refs[-1]
    combine = combine_ref[...]
    high = combine.astype(bf16)
    low = (combine - high.astype(f32)).astype(bf16)
    rows = jnp.concatenate([b[...] for b in blocks], axis=0)
    dims = (((0,), (0,)), ((), ()))
    mixed = lax.dot_general(high, rows, dims, preferred_element_type=f32)
    mixed += lax.dot_general(low, rows, dims, preferred_element_type=f32)
    out_ref[...] = mixed.astype(bf16)


def spread(pieces, m, bit):
    have = [m]
    while bit:
        for k in list(have):
            pieces[k ^ bit] = [swap(g, "pd", bit) for g in pieces[k]]
            have.append(k ^ bit)
        bit //= 2


def on_device(
    tokens,
    expert_ids,
    gate_scores,
    gate_weight,
    up_weight,
    down_weight,
    cache_rows,
    lengths,
    destination,
    decode_query,
):
    ep_count = lax.axis_size("ep")
    pd_count = lax.axis_size("pd")
    token_count, width = tokens.shape
    hidden_units = gate_weight.shape[2]
    slot_count = ep_count * CAP
    half = ep_count // 2

    blocks, combine = route(
        expert_ids.T, gate_scores.T, tokens, cache_rows, destination, ep_count
    )
    arrived = [blocks[0]] + [swap(blocks[d], "ep", d) for d in range(1, ep_count)]
    bit = pd_count // 2
    over = swap(blocks[0], "pd", bit)
    (w_gate,), mark = fetch(combine, gate_weight[0])
    rest = join(arrived[1:], [mark, over])
    (w_up, w_down), mark = fetch(rest, up_weight[0], down_weight[0])

    pieces = {0: [blocks[0], rest]}
    pieces[bit] = [over, swap(rest, "pd", bit)]
    early = list(range(bit))
    late = [m ^ bit for m in early]
    spread(pieces, 0, bit // 2)
    sums = jax.ShapeDtypeStruct((slot_count, hidden_units), f32)
    operands = [g for m in early for g in pieces[m]]
    gate_sums, up_sums = pl.pallas_call(
        functools.partial(first_kernel, early, width),
        out_shape=[sums, sums],
        in_specs=[VMEM] * (2 + len(operands)),
        out_specs=[VMEM, VMEM],
        compiler_params=params(operands * 2),
        cost_estimate=cost(4 * slot_count * w_gate.size * 2, 2 * w_gate.size),
        name="gate_up_first",
    )(w_gate, w_up, *operands)
    pieces[bit][1] = tie(pieces[bit][1], [mark, gate_sums])
    spread(pieces, bit, bit // 2)
    others = sorted([m for m in range(pd_count) if m & 1], reverse=True)
    stay = sorted([m for m in range(pd_count) if not m & 1], reverse=True)
    operands = [g for m in late for g in pieces[m]]
    out_shape = [jax.ShapeDtypeStruct((slot_count, width), bf16)] * len(others)
    out_shape += [jax.ShapeDtypeStruct((slot_count, hidden_units), bf16)]
    outs = pl.pallas_call(
        functools.partial(second_kernel, late, others, width),
        out_shape=out_shape,
        in_specs=[VMEM] * (5 + len(operands)),
        out_specs=[VMEM] * len(out_shape),
        compiler_params=params(operands * 2 + out_shape * 2),
        cost_estimate=cost(6 * slot_count * w_gate.size * 2, 2 * w_gate.size),
        name="gate_up_down",
    )(w_gate, w_up, w_down, gate_sums, up_sums, *operands)
    parts = dict(zip(others, outs[:-1]))
    out_shape = [jax.ShapeDtypeStruct((slot_count, width), f32)] * len(stay)
    outs = pl.pallas_call(
        functools.partial(third_kernel, stay, width),
        out_shape=out_shape,
        in_specs=[VMEM, VMEM],
        out_specs=[VMEM] * len(out_shape),
        compiler_params=params(out_shape * 2),
        cost_estimate=cost(2 * slot_count * w_down.size, w_down.size),
        name="down_rest",
    )(outs[-1], w_down)
    kept = dict(zip(stay, outs))
    cut = half * CAP
    kept = {m: dict(zip((0, cut), total(kept[m], swap(parts[m ^ 1], "pd", 1), 2, f32))) for m in stay}
    returned = [None] * ep_count
    for low in (cut, 0):
        rows = {m: kept[m][low] for m in stay}
        bit = 2
        while bit < pd_count:
            for m in sorted(rows, reverse=True):
                if m & bit:
                    over = swap(rows.pop(m).astype(bf16), "pd", bit)
                    final = bit * 2 == pd_count
                    rows[m ^ bit] = total(rows[m ^ bit], over, half if final else 1, bf16 if final else f32)
                    rows[m ^ bit] = rows[m ^ bit] if final else rows[m ^ bit][0]
            bit *= 2
        for i, block in enumerate(rows[0]):
            d = low // CAP + i
            returned[d] = swap(block, "ep", d) if d else block
    mixed = jax.ShapeDtypeStruct((token_count, width), bf16)
    mixed = pl.pallas_call(
        combine_kernel,
        out_shape=mixed,
        in_specs=[VMEM] * (1 + ep_count),
        out_specs=VMEM,
        compiler_params=params([mixed] * 4),
        cost_estimate=cost(4 * slot_count * tokens.size, 2 * tokens.size),
        name="combine",
    )(combine, *returned)

    operands = [g for m in range(pd_count) for g in pieces[m]]
    attended = jax.ShapeDtypeStruct(decode_query.shape[1:3] + (LATC,), bf16)
    attended = pl.pallas_call(
        functools.partial(attend_kernel, ep_count, pd_count, width),
        out_shape=attended,
        in_specs=[SMEM, SMEM, VMEM] + [VMEM] * len(operands),
        out_specs=VMEM,
        compiler_params=params(operands + [decode_query, attended]),
        cost_estimate=cost(8 * slot_count * tokens.size, 8 * tokens.size),
        name="attend",
    )(destination, lengths, decode_query[0], *operands)
    return (mixed, attended[None])


def solution(mesh):
    in_specs = (
        P(("group", "ep"), "pd"),
        P(("group", "ep"), None),
        P(("group", "ep"), None),
        P("ep", None, "pd"),
        P("ep", None, "pd"),
        P("ep", "pd", None),
        P(("group", "ep"), "pd", None),
        P("group"),
        P("group", None),
        P(("group", "ep"), None, "pd", None),
    )
    out_specs = (P(("group", "ep"), "pd"), P(("group", "ep"), None, "pd", None))
    return jax.shard_map(
        on_device, mesh=mesh, in_specs=in_specs, out_specs=out_specs, check_vma=False
    )
```

```python
import functools

import jax
import jax.numpy as jnp
from jax import lax
from jax.experimental import pallas as pl
from jax.experimental.pallas import tpu as pltpu
from jax.sharding import PartitionSpec as P

LATC = 512
CAP = 16

score_scale = 192.0 ** (-0.5)

bf16, f32, i32 = jnp.bfloat16, jnp.float32, jnp.int32
VMEM = pl.BlockSpec(memory_space=pltpu.VMEM)
SMEM = pl.BlockSpec(memory_space=pltpu.SMEM)
HBM = pl.BlockSpec(memory_space=pltpu.HBM)
ANY = pl.BlockSpec(memory_space=pl.ANY)


def swap(value, axis, mask):
    count = lax.axis_size(axis)
    return lax.ppermute(value, axis, [(i, i ^ mask) for i in range(count)])


def in_hbm(value):
    return pltpu.with_memory_space_constraint(value, pltpu.HBM)


def params(arrays, extra=6 << 20):
    held = sum(a.size * a.dtype.itemsize for a in arrays)
    return pltpu.CompilerParams(vmem_limit_bytes=min(held + extra, 60 << 20))


def cost(flops, moved=0):
    return pl.CostEstimate(flops=flops, bytes_accessed=moved, transcendentals=0)


def fold_widths(latr):
    first = latr // 2 // 128 * 128
    return first, latr - first, -(-(latr - first) // 128) * 128


def slots_of(ids, own, ep_count):
    token_count = ids.shape[1]
    served = []
    for d in range(ep_count):
        named = jnp.where(ids == (own ^ d), 1.0, 0.0)
        served.append(jnp.sum(named, axis=0, keepdims=True))
    shape = (token_count, token_count)
    earlier = lax.broadcasted_iota(i32, shape, 0) < lax.broadcasted_iota(i32, shape, 1)
    marks = jnp.concatenate(served, axis=0)
    rank = jnp.dot(
        marks.astype(bf16), jnp.where(earlier, 1.0, 0.0).astype(bf16), preferred_element_type=f32
    )
    rank = jnp.where(marks > 0.5, rank, -1.0)
    slots = lax.broadcasted_iota(i32, (CAP, token_count), 0).astype(f32)
    return [slots == rank[d : d + 1] for d in range(ep_count)]


def route_kernel(ep_count, *refs):
    sources, blocks = refs[:4], refs[4 : 4 + ep_count]
    held, sems = refs[4 + ep_count : -1], refs[-1]
    copies = [pltpu.make_async_copy(sources[i], held[i], sems.at[i]) for i in range(4)]
    for copy in copies:
        copy.start()
    ids_ref, dest_ref, cache_ref, tokens_ref = held
    own = lax.axis_index("ep")
    width = tokens_ref.shape[1]
    first, second, wide = fold_widths(cache_ref.shape[2])
    part = cache_ref.shape[1]
    copies[0].wait()
    chosen = slots_of(ids_ref[...], own, ep_count)
    dispatch = jnp.concatenate([jnp.where(c, 1.0, 0.0) for c in chosen], axis=0).astype(bf16)
    copies[1].wait()
    copies[2].wait()
    for d in range(ep_count):
        pick = i32(0)
        for k in range(ep_count):
            pick = jnp.where(dest_ref[own, k] == (own ^ d), k, pick)
        kept = cache_ref[pick].astype(f32)
        above = jnp.concatenate([kept[:, :first], jnp.zeros((part, wide - first), f32)], axis=1)
        below = jnp.concatenate([kept[:, first:], jnp.zeros((part, wide - second), f32)], axis=1)
        blocks[d][:, width:] = jnp.concatenate([above, below], axis=0).astype(bf16)
    copies[3].wait()
    rows = jnp.dot(dispatch, tokens_ref[...], preferred_element_type=f32)
    for d in range(ep_count):
        blocks[d][:, :width] = rows[d * CAP : (d + 1) * CAP].astype(bf16)


def route(ids, tokens, cache_rows, destination, ep_count):
    width = tokens.shape[1]
    wide = fold_widths(cache_rows.shape[2])[2]
    sources = [ids, destination, cache_rows, tokens]
    out_shape = [jax.ShapeDtypeStruct((CAP, width + wide), bf16)] * ep_count
    places = [pltpu.VMEM, pltpu.SMEM, pltpu.VMEM, pltpu.VMEM]
    return pl.pallas_call(
        functools.partial(route_kernel, ep_count),
        out_shape=out_shape,
        in_specs=[HBM] * 4,
        out_specs=[VMEM] * ep_count,
        scratch_shapes=[p(a.shape, a.dtype) for p, a in zip(places, sources)]
        + [pltpu.SemaphoreType.DMA((4,))],
        compiler_params=params(sources * 2 + out_shape * 2),
        cost_estimate=cost(4 * ep_count * CAP * tokens.size, 2 * tokens.size),
        name="route",
    )(*map(in_hbm, sources))


def gates_kernel(ep_count, cuts, ids_ref, gates_ref, *refs):
    mark_ref = refs[-2]
    copies = start_copies(cuts, refs)
    ids, gates, own = ids_ref[...], gates_ref[...], lax.axis_index("ep")
    chosen = slots_of(ids, own, ep_count)
    table = []
    for d in range(ep_count):
        named = ids == (own ^ d)
        gate = jnp.sum(jnp.where(named, gates, 0.0), axis=0, keepdims=True)
        table.append(jnp.where(chosen[d], gate, 0.0))
    table = jnp.concatenate(table, axis=0)
    high = table.astype(bf16).astype(f32)
    mark_ref[...] = jnp.concatenate([high, table - high], axis=0).T.astype(bf16)
    for copy in copies:
        copy.wait()


def start_copies(cuts, refs):
    count, sems = (len(refs) - 2) // 2, refs[-1]
    copies = []
    for i in range(count):
        rows = refs[i].shape[0] // cuts
        for c in range(cuts):
            at = pl.ds(c * rows, rows)
            copies.append(
                pltpu.make_async_copy(refs[i].at[at], refs[count + i].at[at], sems.at[i, c])
            )
    for copy in copies:
        copy.start()
    return copies


def fetch(arrays, ids, gates, ep_count):
    cuts = 4
    mark = jax.ShapeDtypeStruct((ids.shape[1], 2 * ep_count * CAP), bf16)
    outs = pl.pallas_call(
        functools.partial(gates_kernel, ep_count, cuts),
        out_shape=[pltpu.VMEM(a.shape, a.dtype) for a in arrays] + [mark],
        in_specs=[VMEM] * 2 + [HBM] * len(arrays),
        out_specs=[VMEM] * (len(arrays) + 1),
        scratch_shapes=[pltpu.SemaphoreType.DMA((len(arrays), cuts))],
        compiler_params=params([mark] * 4),
        cost_estimate=cost(0, 0),
        name="fetch",
    )(*map(in_hbm, [ids, gates, *arrays]))
    return outs[:-1], outs[-1]


def fetch_part_kernel(part, parts, source_ref, *refs):
    out_ref, sems = refs[-2:]
    rows = source_ref.shape[0] // parts // 2
    copies = []
    for c in range(2):
        at = pl.ds(part * 2 * rows + c * rows, rows)
        copies.append(pltpu.make_async_copy(source_ref.at[at], out_ref.at[at], sems.at[c]))
    for copy in copies:
        copy.start()
    for copy in copies:
        copy.wait()


def fetch_part(array, part, parts, after, held=None):
    extra = () if held is None else (held,)
    return pl.pallas_call(
        functools.partial(fetch_part_kernel, part, parts),
        out_shape=pltpu.VMEM(array.shape, array.dtype),
        in_specs=[HBM] + [VMEM] * len(extra) + [ANY] * len(after),
        out_specs=VMEM,
        input_output_aliases={1: 0} if extra else {},
        scratch_shapes=[pltpu.SemaphoreType.DMA((2,))],
        compiler_params=pltpu.CompilerParams(vmem_limit_bytes=1 << 20),
        cost_estimate=cost(0, 0),
        name="fetch_part",
    )(in_hbm(array), *extra, *after)


def join_kernel(count, *refs):
    out_ref, at = refs[-1], 0
    for ref in refs[:count]:
        out_ref[at : at + ref.shape[0], :] = ref[...]
        at += ref.shape[0]


def join(blocks, after=(), weight=0):
    rows = sum(b.shape[0] for b in blocks)
    out_shape = jax.ShapeDtypeStruct((rows, blocks[0].shape[1]), blocks[0].dtype)
    return pl.pallas_call(
        functools.partial(join_kernel, len(blocks)),
        out_shape=out_shape,
        in_specs=[VMEM] * len(blocks) + [ANY] * len(after),
        out_specs=VMEM,
        compiler_params=params([out_shape] * 3, 1 << 20),
        cost_estimate=cost(0, weight),
        name="join",
    )(*blocks, *after)


def tie_kernel(*refs):
    pass


def tie(value, after):
    return pl.pallas_call(
        tie_kernel,
        out_shape=jax.ShapeDtypeStruct(value.shape, value.dtype),
        in_specs=[ANY] * (1 + len(after)),
        out_specs=ANY,
        input_output_aliases={0: 0},
        compiler_params=pltpu.CompilerParams(vmem_limit_bytes=1 << 20),
        cost_estimate=cost(0, 0),
        name="tie",
    )(value, *after)


def total_kernel(kept_ref, arrived_ref, *outs):
    at = 0
    for out in outs:
        rows = pl.ds(at, out.shape[0])
        out[...] = (kept_ref[rows, :] + arrived_ref[rows, :].astype(f32)).astype(out.dtype)
        at += out.shape[0]


def total(kept, arrived, count, dtype=bf16):
    rows, columns = kept.shape
    out_shape = [jax.ShapeDtypeStruct((rows // count, columns), dtype)] * count
    return pl.pallas_call(
        total_kernel,
        out_shape=out_shape,
        in_specs=[VMEM, VMEM],
        out_specs=[VMEM] * count,
        compiler_params=params([kept] * 4, 1 << 20),
        cost_estimate=cost(kept.size, 8 * kept.size),
        name="total",
    )(kept, arrived)


def piece_sums(piece_refs, masks, me, width, gate_ref, up_ref):
    gate_sums = up_sums = None
    for refs, m in zip(piece_refs, masks):
        rows = jnp.concatenate([r[:, :width] for r in refs], axis=0)
        at = pl.ds(pl.multiple_of((me ^ m) * width, width), width)
        g = jnp.dot(rows, gate_ref[at, :], preferred_element_type=f32)
        u = jnp.dot(rows, up_ref[at, :], preferred_element_type=f32)
        gate_sums = g if gate_sums is None else gate_sums + g
        up_sums = u if up_sums is None else up_sums + u
    return gate_sums, up_sums


def gate_up_kernel(masks, width, has_sums, gate_ref, up_ref, *refs):
    before, refs = (refs[:2], refs[2:]) if has_sums else ((), refs)
    pieces, outs = refs[:-2], refs[-2:]
    per = len(pieces) // len(masks)
    groups = [pieces[i * per : (i + 1) * per] for i in range(len(masks))]
    sums = piece_sums(groups, masks, lax.axis_index("pd"), width, gate_ref, up_ref)
    for i in range(2):
        outs[i][...] = sums[i] + before[i][...] if has_sums else sums[i]


def gate_up(masks, width, w_gate, w_up, pieces, before=()):
    operands = [g for m in masks for g in pieces[m]]
    rows = sum(g.shape[0] for g in pieces[masks[0]])
    sums = jax.ShapeDtypeStruct((rows, w_gate.shape[1]), f32)
    return pl.pallas_call(
        functools.partial(gate_up_kernel, masks, width, bool(before)),
        out_shape=[sums, sums],
        in_specs=[VMEM] * (2 + len(before) + len(operands)),
        out_specs=[VMEM, VMEM],
        compiler_params=params(operands * 2),
        cost_estimate=cost(4 * rows * w_gate.size, 4 * w_gate.size),
        name="gate_up",
    )(w_gate, w_up, *before, *operands)


def hidden_kernel(masks, target, width, gate_ref, up_ref, down_ref, *refs):
    (gsum_ref, usum_ref), pieces, (hidden_ref, out_ref) = refs[:2], refs[2:-2], refs[-2:]
    per = len(pieces) // len(masks)
    groups = [pieces[i * per : (i + 1) * per] for i in range(len(masks))]
    me = lax.axis_index("pd")
    gate_sums, up_sums = piece_sums(groups, masks, me, width, gate_ref, up_ref)
    gate_sums, up_sums = gate_sums + gsum_ref[...], up_sums + usum_ref[...]
    hidden = (gate_sums / (1.0 + jnp.exp(-gate_sums)) * up_sums).astype(bf16)
    hidden_ref[...] = hidden
    at = pl.ds(pl.multiple_of((me ^ target) * width, width), width)
    out_ref[...] = jnp.dot(hidden, down_ref[:, at], preferred_element_type=f32).astype(bf16)


def hidden_units_of(masks, target, width, w_gate, w_up, w_down, sums, pieces):
    operands = [g for m in masks for g in pieces[m]]
    rows, units = sums[0].shape
    out_shape = [jax.ShapeDtypeStruct((rows, n), bf16) for n in (units, width)]
    return pl.pallas_call(
        functools.partial(hidden_kernel, masks, target, width),
        out_shape=out_shape,
        in_specs=[VMEM] * (5 + len(operands)),
        out_specs=[VMEM] * 2,
        compiler_params=params(operands * 2 + out_shape * 2),
        cost_estimate=cost(6 * rows * w_gate.size, 4 * w_gate.size),
        name="hidden",
    )(w_gate, w_up, w_down, *sums, *operands)


def down_kernel(targets, width, hidden_ref, down_ref, *outs):
    me = lax.axis_index("pd")
    for out, m in zip(outs, targets):
        at = pl.ds(pl.multiple_of((me ^ m) * width, width), width)
        product = jnp.dot(hidden_ref[...], down_ref[:, at], preferred_element_type=f32)
        out[...] = product.astype(out.dtype)


def down(targets, width, hidden, w_down, dtype):
    out_shape = [jax.ShapeDtypeStruct((hidden.shape[0], width), dtype)] * len(targets)
    return pl.pallas_call(
        functools.partial(down_kernel, targets, width),
        out_shape=out_shape,
        in_specs=[VMEM, VMEM],
        out_specs=[VMEM] * len(out_shape),
        compiler_params=params(out_shape * 2),
        cost_estimate=cost(2 * hidden.shape[0] * w_down.size, 2 * w_down.size),
        name="down",
    )(hidden, w_down)


def attend_kernel(ep_count, pd_count, width, dest_ref, len_ref, query_ref, *refs):
    pieces, out_ref = refs[:-1], refs[-1]
    per = len(pieces) // pd_count
    own, me = lax.axis_index("ep"), lax.axis_index("pd")
    rows, latr = query_ref.shape
    first, second, wide = fold_widths(latr)
    part, heads = CAP // 2, rows // ep_count
    keys = []
    for ref in pieces:
        count = ref.shape[0] // CAP
        folded = ref[:, width:].astype(f32).reshape(count, CAP, wide)
        whole = jnp.concatenate([folded[:, :part, :first], folded[:, part:, :second]], axis=2)
        keys.append(whole.reshape(count * part, latr))
    keys = jnp.concatenate(keys, axis=0).astype(bf16)
    shape = (1, keys.shape[0])
    column = lax.broadcasted_iota(i32, shape, 1)
    block = column // part % ep_count
    position = (me ^ (column // (part * ep_count))) * part + column % part
    length = jnp.zeros(shape, i32)
    for d in range(ep_count):
        j = own ^ d
        here = i32(0)
        for k in range(ep_count):
            here = jnp.where(dest_ref[j, k] == own, len_ref[j * ep_count + k], here)
        length = jnp.where(block == d, here, length)
    slot = jnp.where(position < length, own ^ block, -1)
    usable = lax.broadcasted_iota(i32, (rows, 1), 0) // heads == slot
    scores = lax.dot_general(
        query_ref[...], keys, (((1,), (1,)), ((), ())), preferred_element_type=f32
    )
    scores = scores * score_scale
    top = jnp.max(jnp.where(usable, scores, -1e30), axis=1, keepdims=True)
    weights = jnp.where(usable, jnp.exp(scores - top), 0.0)
    total = jnp.sum(weights, axis=1, keepdims=True)
    summed = jnp.dot(weights.astype(bf16), keys[:, :LATC], preferred_element_type=f32)
    out_ref[...] = (summed / total).astype(bf16)


def combine_kernel(cuts, table_ref, *refs):
    blocks, (out_ref, held_ref, sems) = refs[:-3], refs[-3:]
    rows = jnp.concatenate([b[...] for b in blocks] * 2, axis=0)
    table, width = table_ref[...], held_ref.shape[1] // cuts
    copies = []
    for c in range(cuts):
        at = pl.ds(c * width, width)
        mixed = jnp.dot(
            table, rows[:, c * width : (c + 1) * width], preferred_element_type=f32
        )
        held_ref[:, at] = mixed.astype(bf16)
        copies.append(pltpu.make_async_copy(held_ref.at[:, at], out_ref.at[:, at], sems.at[c]))
        copies[-1].start()
    for copy in copies:
        copy.wait()


def mix(table, blocks):
    mixed = jax.ShapeDtypeStruct((table.shape[0], blocks[0].shape[1]), bf16)
    cuts = 2 if mixed.shape[1] % 256 == 0 else 1
    return pl.pallas_call(
        functools.partial(combine_kernel, cuts),
        out_shape=mixed,
        in_specs=[VMEM] * (1 + len(blocks)),
        out_specs=HBM,
        scratch_shapes=[pltpu.VMEM(mixed.shape, bf16), pltpu.SemaphoreType.DMA((cuts,))],
        compiler_params=params([mixed] * 4 + blocks * 2),
        cost_estimate=cost(4 * CAP * len(blocks) * mixed.size, 2 * mixed.size),
        name="combine",
    )(table, *blocks)


def spread(pieces, m, bit):
    have = [m]
    while bit:
        for k in list(have):
            pieces[k ^ bit] = [swap(g, "pd", bit) for g in pieces[k]]
            have.append(k ^ bit)
        bit //= 2


def on_device(
    tokens,
    expert_ids,
    gate_scores,
    gate_weight,
    up_weight,
    down_weight,
    cache_rows,
    lengths,
    destination,
    decode_query,
):
    ep_count = lax.axis_size("ep")
    pd_count = lax.axis_size("pd")
    width = tokens.shape[1]
    half = ep_count // 2
    ids = expert_ids.T

    blocks = route(ids, tokens, cache_rows, destination, ep_count)
    arrived = [blocks[0]] + [swap(blocks[d], "ep", d) for d in range(1, ep_count)]
    bit = pd_count // 2
    over = swap(blocks[0], "pd", bit)
    (w_gate, w_up), table = fetch([gate_weight[0], up_weight[0]], ids, gate_scores.T, ep_count)
    rest = join(arrived[1:], [table, over])
    pieces = {0: [blocks[0], rest]}
    pieces[bit] = [over, swap(rest, "pd", bit)]
    pieces[0][1] = join(arrived[1:], [rest])
    w_down = fetch_part(down_weight[0], 0, 1, pieces[0])
    spread(pieces, 0, bit // 2)
    sums = gate_up([0], width, w_gate, w_up, pieces)
    pieces[bit][1] = tie(pieces[bit][1], [sums[0], w_down])
    spread(pieces, bit, bit // 2)
    sums = gate_up(list(range(1, bit + 1)), width, w_gate, w_up, pieces, before=sums)
    late = list(range(bit + 1, pd_count))
    others = sorted([m for m in range(pd_count) if m & 1], reverse=True)
    stay = sorted([m for m in range(pd_count) if not m & 1], reverse=True)
    hidden, part = hidden_units_of(
        late, others[0], width, w_gate, w_up, w_down, sums, pieces
    )
    parts = {others[0]: part}
    parts.update(zip(others[1:], down(others[1:], width, hidden, w_down, bf16)))
    kept = dict(zip(stay, down(stay, width, hidden, w_down, f32)))
    cut = half * CAP
    for m in stay:
        sent = bf16 if m & 2 else f32
        kept[m] = dict(zip((0, cut), total(kept[m], swap(parts[m ^ 1], "pd", 1), 2, sent)))

    operands = [g for m in range(pd_count) for g in pieces[m]]
    queries = decode_query.reshape(-1, decode_query.shape[3])
    attended = jax.ShapeDtypeStruct((queries.shape[0], LATC), bf16)
    attended = pl.pallas_call(
        functools.partial(attend_kernel, ep_count, pd_count, width),
        out_shape=attended,
        in_specs=[SMEM, SMEM, VMEM] + [VMEM] * len(operands),
        out_specs=VMEM,
        compiler_params=params(operands + [queries, attended] * 4, 12 << 20),
        cost_estimate=cost(8 * CAP * ep_count * tokens.size, 8 * tokens.size),
        name="attend",
    )(*map(in_hbm, [destination, lengths, queries]), *operands)

    returned = [None] * ep_count
    for low in (cut, 0):
        rows = {m: kept[m][low] for m in stay}
        bit = 2
        while bit < pd_count:
            last = bit * 2 == pd_count
            for m in sorted(rows, reverse=True):
                if m & bit:
                    sent = rows.pop(m).astype(bf16)
                    over = swap(sent, "pd", bit)
                    rows[m ^ bit] = total(rows[m ^ bit], over, half if last else 1, bf16 if last else f32)
                    rows[m ^ bit] = rows[m ^ bit] if last else rows[m ^ bit][0]
            bit *= 2
        for i, block in enumerate(rows[0]):
            d = low // CAP + i
            returned[d] = swap(block, "ep", d) if d else block
    mixed = mix(table, returned)
    return (mixed, attended.reshape(decode_query.shape[:3] + (LATC,)))


def solution(mesh):
    in_specs = (
        P(("group", "ep"), "pd"),
        P(("group", "ep"), None),
        P(("group", "ep"), None),
        P("ep", None, "pd"),
        P("ep", None, "pd"),
        P("ep", "pd", None),
        P(("group", "ep"), "pd", None),
        P("group"),
        P("group", None),
        P(("group", "ep"), None, "pd", None),
    )
    out_specs = (P(("group", "ep"), "pd"), P(("group", "ep"), None, "pd", None))
    return jax.shard_map(
        on_device, mesh=mesh, in_specs=in_specs, out_specs=out_specs, check_vma=False
    )
```

```python
import functools

import jax
import jax.numpy as jnp
from jax import lax
from jax.experimental import pallas as pl
from jax.experimental.pallas import tpu as pltpu
from jax.sharding import PartitionSpec as P

LATC = 512
CAP = 16

score_scale = 192.0 ** (-0.5)

bf16, f32, i32 = jnp.bfloat16, jnp.float32, jnp.int32
VMEM = pl.BlockSpec(memory_space=pltpu.VMEM)
SMEM = pl.BlockSpec(memory_space=pltpu.SMEM)
HBM = pl.BlockSpec(memory_space=pltpu.HBM)
ANY = pl.BlockSpec(memory_space=pl.ANY)


def swap(value, axis, mask):
    count = lax.axis_size(axis)
    return lax.ppermute(value, axis, [(i, i ^ mask) for i in range(count)])


def swap_both(value, ep_mask, pd_mask):
    ep_count, pd_count = lax.axis_size("ep"), lax.axis_size("pd")
    pairs = [
        (i * pd_count + j, (i ^ ep_mask) * pd_count + (j ^ pd_mask))
        for i in range(ep_count)
        for j in range(pd_count)
    ]
    return lax.ppermute(value, ("ep", "pd"), pairs)


def in_hbm(value):
    return pltpu.with_memory_space_constraint(value, pltpu.HBM)


def params(arrays, extra=6 << 20):
    held = sum(a.size * a.dtype.itemsize for a in arrays)
    return pltpu.CompilerParams(vmem_limit_bytes=min(held + extra, 60 << 20))


def cost(flops, moved=0):
    return pl.CostEstimate(flops=flops, bytes_accessed=moved, transcendentals=0)


def fold_widths(latr):
    first = latr // 2 // 128 * 128
    return first, latr - first, -(-(latr - first) // 128) * 128


def slots_of(ids, own, ep_count):
    token_count = ids.shape[1]
    served = []
    for d in range(ep_count):
        named = jnp.where(ids == (own ^ d), 1.0, 0.0)
        served.append(jnp.sum(named, axis=0, keepdims=True))
    shape = (token_count, token_count)
    earlier = lax.broadcasted_iota(i32, shape, 0) < lax.broadcasted_iota(i32, shape, 1)
    marks = jnp.concatenate(served, axis=0)
    rank = jnp.dot(
        marks.astype(bf16), jnp.where(earlier, 1.0, 0.0).astype(bf16), preferred_element_type=f32
    )
    rank = jnp.where(marks > 0.5, rank, -1.0)
    slots = lax.broadcasted_iota(i32, (CAP, token_count), 0).astype(f32)
    return [slots == rank[d : d + 1] for d in range(ep_count)]


def route_kernel(ep_count, *refs):
    sources, blocks = refs[:4], refs[4 : 4 + ep_count]
    held, sems = refs[4 + ep_count : -1], refs[-1]
    copies = [pltpu.make_async_copy(sources[i], held[i], sems.at[i]) for i in range(4)]
    for copy in copies:
        copy.start()
    ids_ref, dest_ref, cache_ref, tokens_ref = held
    own = lax.axis_index("ep")
    width = tokens_ref.shape[1]
    first, second, wide = fold_widths(cache_ref.shape[2])
    part = cache_ref.shape[1]
    copies[0].wait()
    chosen = slots_of(ids_ref[...], own, ep_count)
    dispatch = jnp.concatenate([jnp.where(c, 1.0, 0.0) for c in chosen], axis=0).astype(bf16)
    copies[1].wait()
    copies[2].wait()
    for d in range(ep_count):
        pick = i32(0)
        for k in range(ep_count):
            pick = jnp.where(dest_ref[own, k] == (own ^ d), k, pick)
        kept = cache_ref[pick].astype(f32)
        above = jnp.concatenate([kept[:, :first], jnp.zeros((part, wide - first), f32)], axis=1)
        below = jnp.concatenate([kept[:, first:], jnp.zeros((part, wide - second), f32)], axis=1)
        blocks[d][:, width:] = jnp.concatenate([above, below], axis=0).astype(bf16)
    copies[3].wait()
    rows = jnp.dot(dispatch, tokens_ref[...], preferred_element_type=f32)
    for d in range(ep_count):
        blocks[d][:, :width] = rows[d * CAP : (d + 1) * CAP].astype(bf16)


def route(ids, tokens, cache_rows, destination, ep_count):
    width = tokens.shape[1]
    wide = fold_widths(cache_rows.shape[2])[2]
    sources = [ids, destination, cache_rows, tokens]
    out_shape = [jax.ShapeDtypeStruct((CAP, width + wide), bf16)] * ep_count
    places = [pltpu.VMEM, pltpu.SMEM, pltpu.VMEM, pltpu.VMEM]
    return pl.pallas_call(
        functools.partial(route_kernel, ep_count),
        out_shape=out_shape,
        in_specs=[HBM] * 4,
        out_specs=[VMEM] * ep_count,
        scratch_shapes=[p(a.shape, a.dtype) for p, a in zip(places, sources)]
        + [pltpu.SemaphoreType.DMA((4,))],
        compiler_params=params(sources * 2 + out_shape * 2),
        cost_estimate=cost(4 * ep_count * CAP * tokens.size, 2 * tokens.size),
        name="route",
    )(*map(in_hbm, sources))


def gate_table(ids, gates, ep_count):
    own = lax.axis_index("ep")
    chosen = slots_of(ids, own, ep_count)
    table = []
    for d in range(ep_count):
        named = ids == (own ^ d)
        gate = jnp.sum(jnp.where(named, gates, 0.0), axis=0, keepdims=True)
        table.append(jnp.where(chosen[d], gate, 0.0))
    table = jnp.concatenate(table, axis=0)
    high = table.astype(bf16).astype(f32)
    return jnp.concatenate([high, table - high], axis=0).T.astype(bf16)


def fetch_kernel(ep_count, count, skip, *refs):
    sources, outs, sems = refs[:count], refs[skip:-1], refs[-1]
    cuts, copies = sems.shape[1], []
    for i in range(count):
        rows = sources[i].shape[0] // cuts
        for c in range(cuts):
            at = pl.ds(c * rows, rows)
            copies.append(
                pltpu.make_async_copy(sources[i].at[at], outs[i].at[at], sems.at[i, c])
            )
    for copy in copies:
        copy.start()
    if len(outs) > count:
        ids_ref, gates_ref = refs[count : count + 2]
        outs[-1][...] = gate_table(ids_ref[...], gates_ref[...], ep_count)
    for copy in copies:
        copy.wait()


def fetch(arrays, after=(), routing=(), ep_count=0):
    operands = [in_hbm(a) for a in [*arrays, *routing]]
    out_shape = [pltpu.VMEM(a.shape, a.dtype) for a in arrays]
    table = []
    if routing:
        table = [jax.ShapeDtypeStruct((routing[0].shape[1], 2 * ep_count * CAP), bf16)]
    return pl.pallas_call(
        functools.partial(fetch_kernel, ep_count, len(arrays), len(operands) + len(after)),
        out_shape=out_shape + table,
        in_specs=[HBM] * len(arrays) + [VMEM] * len(routing) + [ANY] * len(after),
        out_specs=[VMEM] * len(out_shape + table),
        scratch_shapes=[pltpu.SemaphoreType.DMA((len(arrays), 4))],
        compiler_params=params(table * 4, 1 << 20),
        cost_estimate=cost(0, 0),
        name="fetch",
    )(*operands, *after)


def join_kernel(count, *refs):
    out_ref, at = refs[-1], 0
    for ref in refs[:count]:
        out_ref[at : at + ref.shape[0], :] = ref[...]
        at += ref.shape[0]


def join(blocks, after=(), weight=0):
    rows = sum(b.shape[0] for b in blocks)
    out_shape = jax.ShapeDtypeStruct((rows, blocks[0].shape[1]), blocks[0].dtype)
    return pl.pallas_call(
        functools.partial(join_kernel, len(blocks)),
        out_shape=out_shape,
        in_specs=[VMEM] * len(blocks) + [ANY] * len(after),
        out_specs=VMEM,
        compiler_params=params([out_shape] * 3, 1 << 20),
        cost_estimate=cost(0, weight),
        name="join",
    )(*blocks, *after)


def tie_kernel(*refs):
    pass


def tie(value, after):
    return pl.pallas_call(
        tie_kernel,
        out_shape=jax.ShapeDtypeStruct(value.shape, value.dtype),
        in_specs=[ANY] * (1 + len(after)),
        out_specs=ANY,
        input_output_aliases={0: 0},
        compiler_params=pltpu.CompilerParams(vmem_limit_bytes=1 << 20),
        cost_estimate=cost(0, 0),
        name="tie",
    )(value, *after)


def total_kernel(cuts, kept_ref, arrived_ref, *outs):
    for out, at in zip(outs, cuts):
        rows = pl.ds(at, out.shape[0])
        out[...] = (kept_ref[rows, :].astype(f32) + arrived_ref[rows, :].astype(f32)).astype(out.dtype)


def total(kept, arrived, pieces):
    out_shape = [jax.ShapeDtypeStruct((rows, kept.shape[1]), dtype) for _, rows, dtype in pieces]
    return pl.pallas_call(
        functools.partial(total_kernel, [at for at, _, _ in pieces]),
        out_shape=out_shape,
        in_specs=[VMEM, VMEM],
        out_specs=[VMEM] * len(out_shape),
        compiler_params=params([kept] * 4, 1 << 20),
        cost_estimate=cost(0, 0),
        name="total",
    )(kept, arrived)


def piece_sums(piece_refs, masks, me, width, gate_ref, up_ref):
    gate_sums = up_sums = None
    for refs, m in zip(piece_refs, masks):
        rows = jnp.concatenate([r[:, :width] for r in refs], axis=0)
        at = pl.ds(pl.multiple_of((me ^ m) * width, width), width)
        g = jnp.dot(rows, gate_ref[at, :], preferred_element_type=f32)
        u = jnp.dot(rows, up_ref[at, :], preferred_element_type=f32)
        gate_sums = g if gate_sums is None else gate_sums + g
        up_sums = u if up_sums is None else up_sums + u
    return gate_sums, up_sums


def gate_up_kernel(masks, width, has_sums, gate_ref, up_ref, *refs):
    before, refs = (refs[:2], refs[2:]) if has_sums else ((), refs)
    pieces, outs = refs[:-2], refs[-2:]
    per = len(pieces) // len(masks)
    groups = [pieces[i * per : (i + 1) * per] for i in range(len(masks))]
    sums = piece_sums(groups, masks, lax.axis_index("pd"), width, gate_ref, up_ref)
    for i in range(2):
        outs[i][...] = sums[i] + before[i][...] if has_sums else sums[i]


def gate_up(masks, width, w_gate, w_up, pieces, before=()):
    operands = [g for m in masks for g in pieces[m]]
    rows = sum(g.shape[0] for g in pieces[masks[0]])
    sums = jax.ShapeDtypeStruct((rows, w_gate.shape[1]), f32)
    return pl.pallas_call(
        functools.partial(gate_up_kernel, masks, width, bool(before)),
        out_shape=[sums, sums],
        in_specs=[VMEM] * (2 + len(before) + len(operands)),
        out_specs=[VMEM, VMEM],
        compiler_params=params(operands * 2),
        cost_estimate=cost(0, 0),
        name="gate_up",
    )(w_gate, w_up, *before, *operands)


def hidden_kernel(masks, target, width, gate_ref, up_ref, down_ref, *refs):
    (gsum_ref, usum_ref), pieces, (hidden_ref, out_ref) = refs[:2], refs[2:-2], refs[-2:]
    per = len(pieces) // len(masks)
    groups = [pieces[i * per : (i + 1) * per] for i in range(len(masks))]
    me = lax.axis_index("pd")
    gate_sums, up_sums = piece_sums(groups, masks, me, width, gate_ref, up_ref)
    gate_sums, up_sums = gate_sums + gsum_ref[...], up_sums + usum_ref[...]
    hidden = (gate_sums / (1.0 + jnp.exp(-gate_sums)) * up_sums).astype(bf16)
    hidden_ref[...] = hidden
    at = pl.ds(pl.multiple_of((me ^ target) * width, width), width)
    out_ref[...] = jnp.dot(hidden, down_ref[:, at], preferred_element_type=f32).astype(bf16)


def hidden_units_of(masks, target, width, w_gate, w_up, w_down, sums, pieces):
    operands = [g for m in masks for g in pieces[m]]
    rows, units = sums[0].shape
    out_shape = [jax.ShapeDtypeStruct((rows, n), bf16) for n in (units, width)]
    return pl.pallas_call(
        functools.partial(hidden_kernel, masks, target, width),
        out_shape=out_shape,
        in_specs=[VMEM] * (5 + len(operands)),
        out_specs=[VMEM] * 2,
        compiler_params=params(operands * 2 + out_shape * 2),
        cost_estimate=cost(0, 0),
        name="hidden",
    )(w_gate, w_up, w_down, *sums, *operands)


def down_kernel(targets, width, hidden_ref, down_ref, *outs):
    me = lax.axis_index("pd")
    for out, m in zip(outs, targets):
        at = pl.ds(pl.multiple_of((me ^ m) * width, width), width)
        product = jnp.dot(hidden_ref[...], down_ref[:, at], preferred_element_type=f32)
        out[...] = product.astype(out.dtype)


def down(targets, width, hidden, w_down, dtype):
    out_shape = [jax.ShapeDtypeStruct((hidden.shape[0], width), dtype)] * len(targets)
    return pl.pallas_call(
        functools.partial(down_kernel, targets, width),
        out_shape=out_shape,
        in_specs=[VMEM, VMEM],
        out_specs=[VMEM] * len(out_shape),
        compiler_params=params(out_shape * 2),
        cost_estimate=cost(2 * hidden.shape[0] * w_down.size, 2 * w_down.size),
        name="down",
    )(hidden, w_down)


def attend_kernel(ep_count, pd_count, width, dest_ref, len_ref, query_ref, *refs):
    pieces, out_ref = refs[:-1], refs[-1]
    per = len(pieces) // pd_count
    own, me = lax.axis_index("ep"), lax.axis_index("pd")
    rows, latr = query_ref.shape
    first, second, wide = fold_widths(latr)
    part, heads = CAP // 2, rows // ep_count
    keys = []
    for ref in pieces:
        count = ref.shape[0] // CAP
        folded = ref[:, width:].astype(f32).reshape(count, CAP, wide)
        whole = jnp.concatenate([folded[:, :part, :first], folded[:, part:, :second]], axis=2)
        keys.append(whole.reshape(count * part, latr))
    keys = jnp.concatenate(keys, axis=0).astype(bf16)
    shape = (1, keys.shape[0])
    column = lax.broadcasted_iota(i32, shape, 1)
    block = column // part % ep_count
    position = (me ^ (column // (part * ep_count))) * part + column % part
    length = jnp.zeros(shape, i32)
    for d in range(ep_count):
        j = own ^ d
        here = i32(0)
        for k in range(ep_count):
            here = jnp.where(dest_ref[j, k] == own, len_ref[j * ep_count + k], here)
        length = jnp.where(block == d, here, length)
    slot = jnp.where(position < length, own ^ block, -1)
    usable = lax.broadcasted_iota(i32, (rows, 1), 0) // heads == slot
    scores = lax.dot_general(
        query_ref[...], keys, (((1,), (1,)), ((), ())), preferred_element_type=f32
    )
    scores = scores * score_scale
    top = jnp.max(jnp.where(usable, scores, -1e30), axis=1, keepdims=True)
    weights = jnp.where(usable, jnp.exp(scores - top), 0.0)
    total = jnp.sum(weights, axis=1, keepdims=True)
    summed = jnp.dot(weights.astype(bf16), keys[:, :LATC], preferred_element_type=f32)
    out_ref[...] = (summed / total).astype(bf16)


def combine_kernel(cuts, counts, table_ref, *refs):
    blocks, (out_ref, held_ref, sems) = refs[:-3], refs[-3:]
    rows, at = [], 0
    for count in counts:
        block = blocks[at][...]
        if count == 2:
            block = (block.astype(f32) + blocks[at + 1][...].astype(f32)).astype(bf16)
        rows.append(block)
        at += count
    rows = jnp.concatenate(rows * 2, axis=0)
    table, width = table_ref[...], held_ref.shape[1] // cuts
    copies = []
    for c in range(cuts):
        at = pl.ds(c * width, width)
        mixed = jnp.dot(
            table, rows[:, c * width : (c + 1) * width], preferred_element_type=f32
        )
        held_ref[:, at] = mixed.astype(bf16)
        copies.append(pltpu.make_async_copy(held_ref.at[:, at], out_ref.at[:, at], sems.at[c]))
        copies[-1].start()
    for copy in copies:
        copy.wait()


def mix(table, blocks):
    operands = [part for block in blocks for part in block]
    mixed = jax.ShapeDtypeStruct((table.shape[0], operands[0].shape[1]), bf16)
    cuts = 2 if mixed.shape[1] % 256 == 0 else 1
    return pl.pallas_call(
        functools.partial(combine_kernel, cuts, [len(block) for block in blocks]),
        out_shape=mixed,
        in_specs=[VMEM] * (1 + len(operands)),
        out_specs=HBM,
        scratch_shapes=[pltpu.VMEM(mixed.shape, bf16), pltpu.SemaphoreType.DMA((cuts,))],
        compiler_params=params([mixed] * 4 + operands * 2),
        cost_estimate=cost(4 * CAP * len(blocks) * mixed.size, 2 * mixed.size),
        name="combine",
    )(table, *operands)


def spread(pieces, m, bit):
    have = [m]
    while bit:
        for k in list(have):
            pieces[k ^ bit] = [swap(g, "pd", bit) for g in pieces[k]]
            have.append(k ^ bit)
        bit //= 2


def on_device(
    tokens,
    expert_ids,
    gate_scores,
    gate_weight,
    up_weight,
    down_weight,
    cache_rows,
    lengths,
    destination,
    decode_query,
):
    ep_count = lax.axis_size("ep")
    pd_count = lax.axis_size("pd")
    width = tokens.shape[1]
    ids = expert_ids.T

    blocks = route(ids, tokens, cache_rows, destination, ep_count)
    bit = pd_count // 2
    cut_in = cut_out = min(2, ep_count)
    arrived = [blocks[0]] + [swap(blocks[d], "ep", d) for d in range(1, ep_count)]
    over = [swap(blocks[0], "pd", bit)]
    over += [swap_both(blocks[d], d, bit) for d in range(1, cut_in)]
    w_gate, w_up, table = fetch([gate_weight[0], up_weight[0]], [], (ids, gate_scores.T), ep_count)
    rest = join(arrived[cut_in:], [table])

    pieces = {0: [join(arrived[:cut_in], [rest])], bit: [join(over, [rest])]}
    pieces[bit] += [swap(tie(rest, pieces[0] + pieces[bit]), "pd", bit)]
    pieces[0] += [join(arrived[cut_in:], pieces[0])]
    (w_down,) = fetch([down_weight[0]], pieces[0])
    spread(pieces, 0, bit // 2)
    sums = gate_up([0], width, w_gate, w_up, pieces)
    pieces[bit][-1] = tie(pieces[bit][-1], [sums[0], w_down])
    spread(pieces, bit, bit // 2)
    sums = gate_up(list(range(1, bit + 1)), width, w_gate, w_up, pieces, before=sums)
    late = list(range(bit + 1, pd_count))
    others = sorted([m for m in range(pd_count) if m & 1], reverse=True)
    stay = sorted([m for m in range(pd_count) if not m & 1], reverse=True)
    hidden, part = hidden_units_of(
        late, others[0], width, w_gate, w_up, w_down, sums, pieces
    )
    parts = {others[0]: part}
    parts.update(zip(others[1:], down(others[1:], width, hidden, w_down, bf16)))
    kept = dict(zip(stay, down(stay, width, hidden, w_down, f32)))
    direct = range(1, cut_out)
    shares = [(0, CAP)] + [(d * CAP, CAP) for d in direct]
    if cut_out < ep_count:
        shares += [(cut_out * CAP, (ep_count - cut_out) * CAP)]
    for m in stay:
        kinds = [bf16] * len(shares)
        if not m & bit:
            kinds[0] = kinds[-1] = f32
        kept[m] = total(
            kept[m],
            swap(parts[m ^ 1], "pd", 1),
            [(at, rows, kind) for (at, rows), kind in zip(shares, kinds)],
        )
    operands = [g for m in range(pd_count) for g in pieces[m]]
    queries = decode_query.reshape(-1, decode_query.shape[3])
    attended = jax.ShapeDtypeStruct((queries.shape[0], LATC), bf16)
    attended = pl.pallas_call(
        functools.partial(attend_kernel, ep_count, pd_count, width),
        out_shape=attended,
        in_specs=[SMEM, SMEM, VMEM] + [VMEM] * len(operands),
        out_specs=VMEM,
        compiler_params=params(operands + [queries, attended] * 4, 12 << 20),
        cost_estimate=cost(8 * CAP * ep_count * tokens.size, 8 * tokens.size),
        name="attend",
    )(*map(in_hbm, [destination, lengths, queries]), *operands)

    staged = []
    if cut_out < ep_count:
        staged = total(
            kept[0][-1],
            swap(kept[bit][-1], "pd", bit),
            [(d * CAP, CAP, bf16) for d in range(ep_count - cut_out)],
        )
    returned = [[total(kept[0][0], swap(kept[bit][0], "pd", bit), [(0, CAP, bf16)])[0]]]
    for d in direct:
        returned += [[swap(kept[0][d], "ep", d), swap_both(kept[bit][d], d, bit)]]
    returned += [[swap(block, "ep", cut_out + i)] for i, block in enumerate(staged)]
    mixed = mix(table, returned)
    return (mixed, attended.reshape(decode_query.shape[:3] + (LATC,)))


def solution(mesh):
    in_specs = (
        P(("group", "ep"), "pd"),
        P(("group", "ep"), None),
        P(("group", "ep"), None),
        P("ep", None, "pd"),
        P("ep", None, "pd"),
        P("ep", "pd", None),
        P(("group", "ep"), "pd", None),
        P("group"),
        P("group", None),
        P(("group", "ep"), None, "pd", None),
    )
    out_specs = (P(("group", "ep"), "pd"), P(("group", "ep"), None, "pd", None))
    return jax.shard_map(
        on_device, mesh=mesh, in_specs=in_specs, out_specs=out_specs, check_vma=False
    )
```

```python
import functools

import jax
import jax.numpy as jnp
from jax import lax
from jax.experimental import pallas as pl
from jax.experimental.pallas import tpu as pltpu
from jax.sharding import PartitionSpec as P

LATC = 512
CAP = 16

score_scale = 192.0 ** (-0.5)

bf16, f32, i32 = jnp.bfloat16, jnp.float32, jnp.int32
VMEM = pl.BlockSpec(memory_space=pltpu.VMEM)
SMEM = pl.BlockSpec(memory_space=pltpu.SMEM)
HBM = pl.BlockSpec(memory_space=pltpu.HBM)
ANY = pl.BlockSpec(memory_space=pl.ANY)


def swap(value, axis, mask):
    count = lax.axis_size(axis)
    return lax.ppermute(value, axis, [(i, i ^ mask) for i in range(count)])


def swap_both(value, ep_mask, pd_mask):
    ep_count, pd_count = lax.axis_size("ep"), lax.axis_size("pd")
    pairs = [
        (i * pd_count + j, (i ^ ep_mask) * pd_count + (j ^ pd_mask))
        for i in range(ep_count)
        for j in range(pd_count)
    ]
    return lax.ppermute(value, ("ep", "pd"), pairs)


def in_hbm(value):
    return pltpu.with_memory_space_constraint(value, pltpu.HBM)


def params(arrays, extra=6 << 20):
    held = sum(a.size * a.dtype.itemsize for a in arrays)
    return pltpu.CompilerParams(vmem_limit_bytes=min(held + extra, 60 << 20))


def cost(flops, moved=0):
    return pl.CostEstimate(flops=flops, bytes_accessed=moved, transcendentals=0)


def fold_widths(latr):
    first = latr // 2 // 128 * 128
    return first, latr - first, -(-(latr - first) // 128) * 128


def slots_of(ids, own, ep_count):
    token_count = ids.shape[1]
    served = []
    for d in range(ep_count):
        named = jnp.where(ids == (own ^ d), 1.0, 0.0)
        served.append(jnp.sum(named, axis=0, keepdims=True))
    shape = (token_count, token_count)
    earlier = lax.broadcasted_iota(i32, shape, 0) < lax.broadcasted_iota(i32, shape, 1)
    marks = jnp.concatenate(served, axis=0)
    rank = jnp.dot(
        marks.astype(bf16), jnp.where(earlier, 1.0, 0.0).astype(bf16), preferred_element_type=f32
    )
    rank = jnp.where(marks > 0.5, rank, -1.0)
    slots = lax.broadcasted_iota(i32, (CAP, token_count), 0).astype(f32)
    return [slots == rank[d : d + 1] for d in range(ep_count)]


def route_kernel(ep_count, *refs):
    sources, blocks = refs[:4], refs[4 : 4 + ep_count]
    held, sems = refs[4 + ep_count : -1], refs[-1]
    copies = [pltpu.make_async_copy(sources[i], held[i], sems.at[i]) for i in range(4)]
    for copy in copies:
        copy.start()
    ids_ref, dest_ref, cache_ref, tokens_ref = held
    own = lax.axis_index("ep")
    width = tokens_ref.shape[1]
    first, second, wide = fold_widths(cache_ref.shape[2])
    part = cache_ref.shape[1]
    copies[0].wait()
    chosen = slots_of(ids_ref[...], own, ep_count)
    dispatch = jnp.concatenate([jnp.where(c, 1.0, 0.0) for c in chosen], axis=0).astype(bf16)
    copies[1].wait()
    copies[2].wait()
    for d in range(ep_count):
        pick = i32(0)
        for k in range(ep_count):
            pick = jnp.where(dest_ref[own, k] == (own ^ d), k, pick)
        kept = cache_ref[pick].astype(f32)
        above = jnp.concatenate([kept[:, :first], jnp.zeros((part, wide - first), f32)], axis=1)
        below = jnp.concatenate([kept[:, first:], jnp.zeros((part, wide - second), f32)], axis=1)
        blocks[d][:, width:] = jnp.concatenate([above, below], axis=0).astype(bf16)
    copies[3].wait()
    rows = jnp.dot(dispatch, tokens_ref[...], preferred_element_type=f32)
    for d in range(ep_count):
        blocks[d][:, :width] = rows[d * CAP : (d + 1) * CAP].astype(bf16)


def route(ids, tokens, cache_rows, destination, ep_count):
    width = tokens.shape[1]
    wide = fold_widths(cache_rows.shape[2])[2]
    sources = [ids, destination, cache_rows, tokens]
    out_shape = [jax.ShapeDtypeStruct((CAP, width + wide), bf16)] * ep_count
    places = [pltpu.VMEM, pltpu.SMEM, pltpu.VMEM, pltpu.VMEM]
    return pl.pallas_call(
        functools.partial(route_kernel, ep_count),
        out_shape=out_shape,
        in_specs=[HBM] * 4,
        out_specs=[VMEM] * ep_count,
        scratch_shapes=[p(a.shape, a.dtype) for p, a in zip(places, sources)]
        + [pltpu.SemaphoreType.DMA((4,))],
        compiler_params=params(sources * 2 + out_shape * 2),
        cost_estimate=cost(4 * ep_count * CAP * tokens.size, 2 * tokens.size),
        name="route",
    )(*map(in_hbm, sources))


def gate_table(ids, gates, ep_count):
    own = lax.axis_index("ep")
    chosen = slots_of(ids, own, ep_count)
    table = []
    for d in range(ep_count):
        named = ids == (own ^ d)
        gate = jnp.sum(jnp.where(named, gates, 0.0), axis=0, keepdims=True)
        table.append(jnp.where(chosen[d], gate, 0.0))
    table = jnp.concatenate(table, axis=0)
    high = table.astype(bf16).astype(f32)
    return jnp.concatenate([high, table - high], axis=0).T.astype(bf16)


def fetch_kernel(ep_count, count, skip, *refs):
    sources, outs, sems = refs[:count], refs[skip:-1], refs[-1]
    cuts, copies = sems.shape[1], []
    for i in range(count):
        rows = sources[i].shape[0] // cuts
        for c in range(cuts):
            at = pl.ds(c * rows, rows)
            copies.append(
                pltpu.make_async_copy(sources[i].at[at], outs[i].at[at], sems.at[i, c])
            )
    for copy in copies:
        copy.start()
    if len(outs) > count:
        ids_ref, gates_ref = refs[count : count + 2]
        outs[-1][...] = gate_table(ids_ref[...], gates_ref[...], ep_count)
    for copy in copies:
        copy.wait()


def fetch(arrays, after=(), routing=(), ep_count=0):
    operands = [in_hbm(a) for a in [*arrays, *routing]]
    out_shape = [pltpu.VMEM(a.shape, a.dtype) for a in arrays]
    table = []
    if routing:
        table = [jax.ShapeDtypeStruct((routing[0].shape[1], 2 * ep_count * CAP), bf16)]
    return pl.pallas_call(
        functools.partial(fetch_kernel, ep_count, len(arrays), len(operands) + len(after)),
        out_shape=out_shape + table,
        in_specs=[HBM] * len(arrays) + [VMEM] * len(routing) + [ANY] * len(after),
        out_specs=[VMEM] * len(out_shape + table),
        scratch_shapes=[pltpu.SemaphoreType.DMA((len(arrays), 4))],
        compiler_params=params(table * 4, 1 << 20),
        cost_estimate=cost(0, 0),
        name="fetch",
    )(*operands, *after)


def join_kernel(count, *refs):
    out_ref, at = refs[-1], 0
    for ref in refs[:count]:
        out_ref[at : at + ref.shape[0], :] = ref[...]
        at += ref.shape[0]


def join(blocks, after=(), weight=0):
    rows = sum(b.shape[0] for b in blocks)
    out_shape = jax.ShapeDtypeStruct((rows, blocks[0].shape[1]), blocks[0].dtype)
    return pl.pallas_call(
        functools.partial(join_kernel, len(blocks)),
        out_shape=out_shape,
        in_specs=[VMEM] * len(blocks) + [ANY] * len(after),
        out_specs=VMEM,
        compiler_params=params([out_shape] * 3, 1 << 20),
        cost_estimate=cost(0, weight),
        name="join",
    )(*blocks, *after)


def tie_kernel(*refs):
    pass


def tie(value, after):
    return pl.pallas_call(
        tie_kernel,
        out_shape=jax.ShapeDtypeStruct(value.shape, value.dtype),
        in_specs=[ANY] * (1 + len(after)),
        out_specs=ANY,
        input_output_aliases={0: 0},
        compiler_params=pltpu.CompilerParams(vmem_limit_bytes=1 << 20),
        cost_estimate=cost(0, 0),
        name="tie",
    )(value, *after)


def total_kernel(cuts, kept_ref, arrived_ref, *outs):
    for out, at in zip(outs, cuts):
        rows = pl.ds(at, out.shape[0])
        out[...] = (kept_ref[rows, :].astype(f32) + arrived_ref[rows, :].astype(f32)).astype(out.dtype)


def total(kept, arrived, pieces):
    out_shape = [jax.ShapeDtypeStruct((rows, kept.shape[1]), dtype) for _, rows, dtype in pieces]
    return pl.pallas_call(
        functools.partial(total_kernel, [at for at, _, _ in pieces]),
        out_shape=out_shape,
        in_specs=[VMEM, VMEM],
        out_specs=[VMEM] * len(out_shape),
        compiler_params=params([kept] * 4, 1 << 20),
        cost_estimate=cost(0, 0),
        name="total",
    )(kept, arrived)


def piece_sums(piece_refs, masks, me, width, gate_ref, up_ref):
    gate_sums = up_sums = None
    for refs, m in zip(piece_refs, masks):
        rows = jnp.concatenate([r[:, :width] for r in refs], axis=0)
        at = pl.ds(pl.multiple_of((me ^ m) * width, width), width)
        g = jnp.dot(rows, gate_ref[at, :], preferred_element_type=f32)
        u = jnp.dot(rows, up_ref[at, :], preferred_element_type=f32)
        gate_sums = g if gate_sums is None else gate_sums + g
        up_sums = u if up_sums is None else up_sums + u
    return gate_sums, up_sums


def gate_up_kernel(masks, width, has_sums, gate_ref, up_ref, *refs):
    before, refs = (refs[:2], refs[2:]) if has_sums else ((), refs)
    pieces, outs = refs[:-2], refs[-2:]
    per = len(pieces) // len(masks)
    groups = [pieces[i * per : (i + 1) * per] for i in range(len(masks))]
    sums = piece_sums(groups, masks, lax.axis_index("pd"), width, gate_ref, up_ref)
    for i in range(2):
        outs[i][...] = sums[i] + before[i][...] if has_sums else sums[i]


def gate_up(masks, width, w_gate, w_up, pieces, before=()):
    operands = [g for m in masks for g in pieces[m]]
    rows = sum(g.shape[0] for g in pieces[masks[0]])
    sums = jax.ShapeDtypeStruct((rows, w_gate.shape[1]), f32)
    return pl.pallas_call(
        functools.partial(gate_up_kernel, masks, width, bool(before)),
        out_shape=[sums, sums],
        in_specs=[VMEM] * (2 + len(before) + len(operands)),
        out_specs=[VMEM, VMEM],
        compiler_params=params(operands * 2),
        cost_estimate=cost(0, 0),
        name="gate_up",
    )(w_gate, w_up, *before, *operands)


def hidden_kernel(masks, target, width, gate_ref, up_ref, down_ref, *refs):
    (gsum_ref, usum_ref), pieces, (hidden_ref, out_ref) = refs[:2], refs[2:-2], refs[-2:]
    per = len(pieces) // len(masks)
    groups = [pieces[i * per : (i + 1) * per] for i in range(len(masks))]
    me = lax.axis_index("pd")
    gate_sums, up_sums = piece_sums(groups, masks, me, width, gate_ref, up_ref)
    gate_sums, up_sums = gate_sums + gsum_ref[...], up_sums + usum_ref[...]
    hidden = (gate_sums / (1.0 + jnp.exp(-gate_sums)) * up_sums).astype(bf16)
    hidden_ref[...] = hidden
    at = pl.ds(pl.multiple_of((me ^ target) * width, width), width)
    out_ref[...] = jnp.dot(hidden, down_ref[:, at], preferred_element_type=f32).astype(bf16)


def hidden_units_of(masks, target, width, w_gate, w_up, w_down, sums, pieces):
    operands = [g for m in masks for g in pieces[m]]
    rows, units = sums[0].shape
    out_shape = [jax.ShapeDtypeStruct((rows, n), bf16) for n in (units, width)]
    return pl.pallas_call(
        functools.partial(hidden_kernel, masks, target, width),
        out_shape=out_shape,
        in_specs=[VMEM] * (5 + len(operands)),
        out_specs=[VMEM] * 2,
        compiler_params=params(operands * 2 + out_shape * 2),
        cost_estimate=cost(0, 0),
        name="hidden",
    )(w_gate, w_up, w_down, *sums, *operands)


def down_kernel(targets, width, hidden_ref, down_ref, *outs):
    me = lax.axis_index("pd")
    for out, m in zip(outs, targets):
        at = pl.ds(pl.multiple_of((me ^ m) * width, width), width)
        product = jnp.dot(hidden_ref[...], down_ref[:, at], preferred_element_type=f32)
        out[...] = product.astype(out.dtype)


def down(targets, width, hidden, w_down, dtype):
    out_shape = [jax.ShapeDtypeStruct((hidden.shape[0], width), dtype)] * len(targets)
    return pl.pallas_call(
        functools.partial(down_kernel, targets, width),
        out_shape=out_shape,
        in_specs=[VMEM, VMEM],
        out_specs=[VMEM] * len(out_shape),
        compiler_params=params(out_shape * 2),
        cost_estimate=cost(2 * hidden.shape[0] * w_down.size, 2 * w_down.size),
        name="down",
    )(hidden, w_down)


def attend_kernel(order, pd_count, width, dest_ref, len_ref, query_ref, *refs):
    pieces, out_ref = refs[:-1], refs[-1]
    ep_count = len(order)
    own, me = lax.axis_index("ep"), lax.axis_index("pd")
    rows, latr = query_ref.shape
    first, second, wide = fold_widths(latr)
    part, heads = CAP // 2, rows // ep_count
    keys = []
    for ref in pieces:
        count = ref.shape[0] // CAP
        folded = ref[:, width:].astype(f32).reshape(count, CAP, wide)
        whole = jnp.concatenate([folded[:, :part, :first], folded[:, part:, :second]], axis=2)
        keys.append(whole.reshape(count * part, latr))
    keys = jnp.concatenate(keys, axis=0).astype(bf16)
    shape = (1, keys.shape[0])
    column = lax.broadcasted_iota(i32, shape, 1)
    place = column // part % ep_count
    position = (me ^ (column // (part * ep_count))) * part + column % part
    length, slot = jnp.zeros(shape, i32), jnp.zeros(shape, i32)
    for i, d in enumerate(order):
        j = own ^ d
        here = i32(0)
        for k in range(ep_count):
            here = jnp.where(dest_ref[j, k] == own, len_ref[j * ep_count + k], here)
        length = jnp.where(place == i, here, length)
        slot = jnp.where(place == i, j, slot)
    slot = jnp.where(position < length, slot, -1)
    usable = lax.broadcasted_iota(i32, (rows, 1), 0) // heads == slot
    scores = lax.dot_general(
        query_ref[...], keys, (((1,), (1,)), ((), ())), preferred_element_type=f32
    )
    scores = scores * score_scale
    top = jnp.max(jnp.where(usable, scores, -1e30), axis=1, keepdims=True)
    weights = jnp.where(usable, jnp.exp(scores - top), 0.0)
    total = jnp.sum(weights, axis=1, keepdims=True)
    summed = jnp.dot(weights.astype(bf16), keys[:, :LATC], preferred_element_type=f32)
    out_ref[...] = (summed / total).astype(bf16)


def combine_kernel(cuts, counts, table_ref, *refs):
    blocks, (out_ref, held_ref, sems) = refs[:-3], refs[-3:]
    rows, at = [], 0
    for count in counts:
        block = blocks[at][...]
        if count == 2:
            block = (block.astype(f32) + blocks[at + 1][...].astype(f32)).astype(bf16)
        rows.append(block)
        at += count
    rows = jnp.concatenate(rows * 2, axis=0)
    table, width = table_ref[...], held_ref.shape[1] // cuts
    copies = []
    for c in range(cuts):
        at = pl.ds(c * width, width)
        mixed = jnp.dot(
            table, rows[:, c * width : (c + 1) * width], preferred_element_type=f32
        )
        held_ref[:, at] = mixed.astype(bf16)
        copies.append(pltpu.make_async_copy(held_ref.at[:, at], out_ref.at[:, at], sems.at[c]))
        copies[-1].start()
    for copy in copies:
        copy.wait()


def mix(table, blocks):
    operands = [part for block in blocks for part in block]
    mixed = jax.ShapeDtypeStruct((table.shape[0], operands[0].shape[1]), bf16)
    cuts = 2 if mixed.shape[1] % 256 == 0 else 1
    return pl.pallas_call(
        functools.partial(combine_kernel, cuts, [len(block) for block in blocks]),
        out_shape=mixed,
        in_specs=[VMEM] * (1 + len(operands)),
        out_specs=HBM,
        scratch_shapes=[pltpu.VMEM(mixed.shape, bf16), pltpu.SemaphoreType.DMA((cuts,))],
        compiler_params=params([mixed] * 4 + operands * 2),
        cost_estimate=cost(4 * CAP * len(blocks) * mixed.size, 2 * mixed.size),
        name="combine",
    )(table, *operands)


def spread(pieces, m, bit):
    have = [m]
    while bit:
        for k in list(have):
            pieces[k ^ bit] = [swap(g, "pd", bit) for g in pieces[k]]
            have.append(k ^ bit)
        bit //= 2


def on_device(
    tokens,
    expert_ids,
    gate_scores,
    gate_weight,
    up_weight,
    down_weight,
    cache_rows,
    lengths,
    destination,
    decode_query,
):
    ep_count = lax.axis_size("ep")
    pd_count = lax.axis_size("pd")
    width = tokens.shape[1]
    ids = expert_ids.T

    blocks = route(ids, tokens, cache_rows, destination, ep_count)
    bit = pd_count // 2
    direct = [1]
    staged = [d for d in range(1, ep_count) if d not in direct]
    order = [0, *direct, *staged]
    arrived = [blocks[0]] + [swap(blocks[d], "ep", d) for d in range(1, ep_count)]
    over = [swap(blocks[0], "pd", bit)] + [swap_both(blocks[d], d, bit) for d in direct]
    w_gate, w_up, table = fetch(
        [gate_weight[0], up_weight[0]], [], (ids, gate_scores.T), ep_count
    )
    rest = join([arrived[d] for d in staged], [table])

    pieces = {0: [join([arrived[d] for d in [0, *direct]], [rest])], bit: [join(over, [rest])]}
    pieces[bit] += [swap(tie(rest, pieces[0] + pieces[bit]), "pd", bit)]
    pieces[0] += [join([arrived[d] for d in staged], pieces[0])]
    (w_down,) = fetch([down_weight[0]], pieces[0])
    spread(pieces, 0, bit // 2)
    sums = gate_up([0], width, w_gate, w_up, pieces)
    pieces[bit][-1] = tie(pieces[bit][-1], [sums[0], w_down])
    spread(pieces, bit, bit // 2)
    sums = gate_up(list(range(1, bit + 1)), width, w_gate, w_up, pieces, before=sums)
    late = list(range(bit + 1, pd_count))
    others = sorted([m for m in range(pd_count) if m & 1], reverse=True)
    stay = sorted([m for m in range(pd_count) if not m & 1], reverse=True)
    hidden, part = hidden_units_of(
        late, others[0], width, w_gate, w_up, w_down, sums, pieces
    )
    parts = {others[0]: part}
    parts.update(zip(others[1:], down(others[1:], width, hidden, w_down, bf16)))
    kept = dict(zip(stay, down(stay, width, hidden, w_down, f32)))
    direct = [ep_count - 1]
    summed = [d for d in order if d and d not in direct]
    groups = [[d] for d in direct] + [[0], summed]
    shares = [(order.index(group[0]) * CAP, len(group) * CAP) for group in groups]
    for m in stay:
        kinds = [bf16 if m & bit or i < len(direct) else f32 for i in range(len(groups))]
        kept[m] = total(
            kept[m],
            swap(parts[m ^ 1], "pd", 1),
            [(at, rows, kind) for (at, rows), kind in zip(shares, kinds)],
        )
    operands = [g for m in range(pd_count) for g in pieces[m]]
    queries = decode_query.reshape(-1, decode_query.shape[3])
    attended = jax.ShapeDtypeStruct((queries.shape[0], LATC), bf16)
    attended = pl.pallas_call(
        functools.partial(attend_kernel, order, pd_count, width),
        out_shape=attended,
        in_specs=[SMEM, SMEM, VMEM] + [VMEM] * len(operands),
        out_specs=VMEM,
        compiler_params=params(operands + [queries, attended] * 4, 12 << 20),
        cost_estimate=cost(8 * CAP * ep_count * tokens.size, 8 * tokens.size),
        name="attend",
    )(*map(in_hbm, [destination, lengths, queries]), *operands)

    staged = total(
        kept[0][-1],
        swap(kept[bit][-1], "pd", bit),
        [(i * CAP, CAP, bf16) for i in range(len(summed))],
    )
    returned = {d: [swap(block, "ep", d)] for d, block in zip(summed, staged)}
    for i, d in enumerate(direct):
        returned[d] = [swap(kept[0][i], "ep", d), swap_both(kept[bit][i], d, bit)]
    returned[0] = total(kept[0][-2], swap(kept[bit][-2], "pd", bit), [(0, CAP, bf16)])
    returned = [returned[d] for d in range(ep_count)]
    mixed = mix(table, returned)
    return (mixed, attended.reshape(decode_query.shape[:3] + (LATC,)))


def solution(mesh):
    in_specs = (
        P(("group", "ep"), "pd"),
        P(("group", "ep"), None),
        P(("group", "ep"), None),
        P("ep", None, "pd"),
        P("ep", None, "pd"),
        P("ep", "pd", None),
        P(("group", "ep"), "pd", None),
        P("group"),
        P("group", None),
        P(("group", "ep"), None, "pd", None),
    )
    out_specs = (P(("group", "ep"), "pd"), P(("group", "ep"), None, "pd", None))
    return jax.shard_map(
        on_device, mesh=mesh, in_specs=in_specs, out_specs=out_specs, check_vma=False
    )
```

```python
import functools

import jax
import jax.numpy as jnp
from jax import lax
from jax.experimental import pallas as pl
from jax.experimental.pallas import tpu as pltpu
from jax.sharding import PartitionSpec as P

LATC = 512
CAP = 16

score_scale = 192.0 ** (-0.5)

bf16, f32, i32 = jnp.bfloat16, jnp.float32, jnp.int32
VMEM = pl.BlockSpec(memory_space=pltpu.VMEM)
SMEM = pl.BlockSpec(memory_space=pltpu.SMEM)
HBM = pl.BlockSpec(memory_space=pltpu.HBM)
ANY = pl.BlockSpec(memory_space=pl.ANY)


def swap(value, axis, mask):
    count = lax.axis_size(axis)
    return lax.ppermute(value, axis, [(i, i ^ mask) for i in range(count)])


def swap_both(value, ep_mask, pd_mask):
    ep_count, pd_count = lax.axis_size("ep"), lax.axis_size("pd")
    pairs = [
        (i * pd_count + j, (i ^ ep_mask) * pd_count + (j ^ pd_mask))
        for i in range(ep_count)
        for j in range(pd_count)
    ]
    return lax.ppermute(value, ("ep", "pd"), pairs)


def in_hbm(value):
    return pltpu.with_memory_space_constraint(value, pltpu.HBM)


def params(arrays, extra=6 << 20):
    held = sum(a.size * a.dtype.itemsize for a in arrays)
    return pltpu.CompilerParams(vmem_limit_bytes=min(held + extra, 60 << 20))


def cost(flops, moved=0):
    return pl.CostEstimate(flops=flops, bytes_accessed=moved, transcendentals=0)


def fold_widths(latr):
    first = latr // 2 // 128 * 128
    return first, latr - first, -(-(latr - first) // 128) * 128


def slots_of(ids, own, ep_count):
    token_count = ids.shape[1]
    served = []
    for d in range(ep_count):
        named = jnp.where(ids == (own ^ d), 1.0, 0.0)
        served.append(jnp.sum(named, axis=0, keepdims=True))
    shape = (token_count, token_count)
    earlier = lax.broadcasted_iota(i32, shape, 0) < lax.broadcasted_iota(i32, shape, 1)
    marks = jnp.concatenate(served, axis=0)
    rank = jnp.dot(
        marks.astype(bf16), jnp.where(earlier, 1.0, 0.0).astype(bf16), preferred_element_type=f32
    )
    rank = jnp.where(marks > 0.5, rank, -1.0)
    slots = lax.broadcasted_iota(i32, (CAP, token_count), 0).astype(f32)
    return [slots == rank[d : d + 1] for d in range(ep_count)]


def route_kernel(ep_count, *refs):
    sources, blocks = refs[:4], refs[4 : 4 + ep_count]
    held, sems = refs[4 + ep_count : -1], refs[-1]
    copies = [pltpu.make_async_copy(sources[i], held[i], sems.at[i]) for i in range(4)]
    for copy in copies:
        copy.start()
    ids_ref, dest_ref, cache_ref, tokens_ref = held
    own = lax.axis_index("ep")
    width = tokens_ref.shape[1]
    first, second, wide = fold_widths(cache_ref.shape[2])
    part = cache_ref.shape[1]
    copies[0].wait()
    chosen = slots_of(ids_ref[...], own, ep_count)
    dispatch = jnp.concatenate([jnp.where(c, 1.0, 0.0) for c in chosen], axis=0).astype(bf16)
    copies[1].wait()
    copies[2].wait()
    for d in range(ep_count):
        pick = i32(0)
        for k in range(ep_count):
            pick = jnp.where(dest_ref[own, k] == (own ^ d), k, pick)
        kept = cache_ref[pick].astype(f32)
        above = jnp.concatenate([kept[:, :first], jnp.zeros((part, wide - first), f32)], axis=1)
        below = jnp.concatenate([kept[:, first:], jnp.zeros((part, wide - second), f32)], axis=1)
        blocks[d][:, width:] = jnp.concatenate([above, below], axis=0).astype(bf16)
    copies[3].wait()
    rows = jnp.dot(dispatch, tokens_ref[...], preferred_element_type=f32)
    for d in range(ep_count):
        blocks[d][:, :width] = rows[d * CAP : (d + 1) * CAP].astype(bf16)


def route(ids, tokens, cache_rows, destination, ep_count):
    width = tokens.shape[1]
    wide = fold_widths(cache_rows.shape[2])[2]
    sources = [ids, destination, cache_rows, tokens]
    out_shape = [jax.ShapeDtypeStruct((CAP, width + wide), bf16)] * ep_count
    places = [pltpu.VMEM, pltpu.SMEM, pltpu.VMEM, pltpu.VMEM]
    return pl.pallas_call(
        functools.partial(route_kernel, ep_count),
        out_shape=out_shape,
        in_specs=[HBM] * 4,
        out_specs=[VMEM] * ep_count,
        scratch_shapes=[p(a.shape, a.dtype) for p, a in zip(places, sources)]
        + [pltpu.SemaphoreType.DMA((4,))],
        compiler_params=params(sources * 2 + out_shape * 2),
        cost_estimate=cost(4 * ep_count * CAP * tokens.size, 2 * tokens.size),
        name="route",
    )(*map(in_hbm, sources))


def gate_table(ids, gates, ep_count):
    own = lax.axis_index("ep")
    chosen = slots_of(ids, own, ep_count)
    table = []
    for d in range(ep_count):
        named = ids == (own ^ d)
        gate = jnp.sum(jnp.where(named, gates, 0.0), axis=0, keepdims=True)
        table.append(jnp.where(chosen[d], gate, 0.0))
    table = jnp.concatenate(table, axis=0)
    high = table.astype(bf16).astype(f32)
    return jnp.concatenate([high, table - high], axis=0).T.astype(bf16)


def fetch_kernel(ep_count, count, skip, *refs):
    sources, outs, sems = refs[:count], refs[skip:-1], refs[-1]
    cuts, copies = sems.shape[1], []
    for i in range(count):
        rows = sources[i].shape[0] // cuts
        for c in range(cuts):
            at = pl.ds(c * rows, rows)
            copies.append(
                pltpu.make_async_copy(sources[i].at[at], outs[i].at[at], sems.at[i, c])
            )
    for copy in copies:
        copy.start()
    if len(outs) > count:
        ids_ref, gates_ref = refs[count : count + 2]
        outs[-1][...] = gate_table(ids_ref[...], gates_ref[...], ep_count)
    for copy in copies:
        copy.wait()


def fetch(arrays, after=(), routing=(), ep_count=0):
    operands = [in_hbm(a) for a in [*arrays, *routing]]
    out_shape = [pltpu.VMEM(a.shape, a.dtype) for a in arrays]
    table = []
    if routing:
        table = [jax.ShapeDtypeStruct((routing[0].shape[1], 2 * ep_count * CAP), bf16)]
    return pl.pallas_call(
        functools.partial(fetch_kernel, ep_count, len(arrays), len(operands) + len(after)),
        out_shape=out_shape + table,
        in_specs=[HBM] * len(arrays) + [VMEM] * len(routing) + [ANY] * len(after),
        out_specs=[VMEM] * len(out_shape + table),
        scratch_shapes=[pltpu.SemaphoreType.DMA((len(arrays), 4))],
        compiler_params=params(table * 4, 1 << 20),
        cost_estimate=cost(0, 0),
        name="fetch",
    )(*operands, *after)


def join_kernel(count, *refs):
    out_ref, at = refs[-1], 0
    for ref in refs[:count]:
        out_ref[at : at + ref.shape[0], :] = ref[...]
        at += ref.shape[0]


def join(blocks, after=(), weight=0):
    rows = sum(b.shape[0] for b in blocks)
    out_shape = jax.ShapeDtypeStruct((rows, blocks[0].shape[1]), blocks[0].dtype)
    return pl.pallas_call(
        functools.partial(join_kernel, len(blocks)),
        out_shape=out_shape,
        in_specs=[VMEM] * len(blocks) + [ANY] * len(after),
        out_specs=VMEM,
        compiler_params=params([out_shape] * 3, 1 << 20),
        cost_estimate=cost(0, weight),
        name="join",
    )(*blocks, *after)


def tie_kernel(*refs):
    pass


def tie(value, after):
    return pl.pallas_call(
        tie_kernel,
        out_shape=jax.ShapeDtypeStruct(value.shape, value.dtype),
        in_specs=[ANY] * (1 + len(after)),
        out_specs=ANY,
        input_output_aliases={0: 0},
        compiler_params=pltpu.CompilerParams(vmem_limit_bytes=1 << 20),
        cost_estimate=cost(0, 0),
        name="tie",
    )(value, *after)


def total_kernel(cuts, kept_ref, arrived_ref, *outs):
    for out, at in zip(outs, cuts):
        rows = pl.ds(at, out.shape[0])
        out[...] = (kept_ref[rows, :].astype(f32) + arrived_ref[rows, :].astype(f32)).astype(out.dtype)


def total(kept, arrived, pieces):
    out_shape = [jax.ShapeDtypeStruct((rows, kept.shape[1]), dtype) for _, rows, dtype in pieces]
    return pl.pallas_call(
        functools.partial(total_kernel, [at for at, _, _ in pieces]),
        out_shape=out_shape,
        in_specs=[VMEM, VMEM],
        out_specs=[VMEM] * len(out_shape),
        compiler_params=params([kept] * 4, 1 << 20),
        cost_estimate=cost(0, 0),
        name="total",
    )(kept, arrived)


def piece_sums(piece_refs, masks, me, width, gate_ref, up_ref):
    gate_sums = up_sums = None
    for refs, m in zip(piece_refs, masks):
        rows = jnp.concatenate([r[:, :width] for r in refs], axis=0)
        at = pl.ds(pl.multiple_of((me ^ m) * width, width), width)
        g = jnp.dot(rows, gate_ref[at, :], preferred_element_type=f32)
        u = jnp.dot(rows, up_ref[at, :], preferred_element_type=f32)
        gate_sums = g if gate_sums is None else gate_sums + g
        up_sums = u if up_sums is None else up_sums + u
    return gate_sums, up_sums


def gate_up_kernel(masks, width, has_sums, gate_ref, up_ref, *refs):
    before, refs = (refs[:2], refs[2:]) if has_sums else ((), refs)
    pieces, outs = refs[:-2], refs[-2:]
    per = len(pieces) // len(masks)
    groups = [pieces[i * per : (i + 1) * per] for i in range(len(masks))]
    sums = piece_sums(groups, masks, lax.axis_index("pd"), width, gate_ref, up_ref)
    for i in range(2):
        outs[i][...] = sums[i] + before[i][...] if has_sums else sums[i]


def gate_up(masks, width, w_gate, w_up, pieces, before=()):
    operands = [g for m in masks for g in pieces[m]]
    rows = sum(g.shape[0] for g in pieces[masks[0]])
    sums = jax.ShapeDtypeStruct((rows, w_gate.shape[1]), f32)
    return pl.pallas_call(
        functools.partial(gate_up_kernel, masks, width, bool(before)),
        out_shape=[sums, sums],
        in_specs=[VMEM] * (2 + len(before) + len(operands)),
        out_specs=[VMEM, VMEM],
        compiler_params=params(operands * 2),
        cost_estimate=cost(0, 0),
        name="gate_up",
    )(w_gate, w_up, *before, *operands)


def hidden_kernel(masks, target, width, gate_ref, up_ref, down_ref, *refs):
    (gsum_ref, usum_ref), pieces, (hidden_ref, out_ref) = refs[:2], refs[2:-2], refs[-2:]
    per = len(pieces) // len(masks)
    groups = [pieces[i * per : (i + 1) * per] for i in range(len(masks))]
    me = lax.axis_index("pd")
    gate_sums, up_sums = piece_sums(groups, masks, me, width, gate_ref, up_ref)
    gate_sums, up_sums = gate_sums + gsum_ref[...], up_sums + usum_ref[...]
    hidden = (gate_sums / (1.0 + jnp.exp(-gate_sums)) * up_sums).astype(bf16)
    hidden_ref[...] = hidden
    at = pl.ds(pl.multiple_of((me ^ target) * width, width), width)
    out_ref[...] = jnp.dot(hidden, down_ref[:, at], preferred_element_type=f32).astype(bf16)


def hidden_units_of(masks, target, width, w_gate, w_up, w_down, sums, pieces):
    operands = [g for m in masks for g in pieces[m]]
    rows, units = sums[0].shape
    out_shape = [jax.ShapeDtypeStruct((rows, n), bf16) for n in (units, width)]
    return pl.pallas_call(
        functools.partial(hidden_kernel, masks, target, width),
        out_shape=out_shape,
        in_specs=[VMEM] * (5 + len(operands)),
        out_specs=[VMEM] * 2,
        compiler_params=params(operands * 2 + out_shape * 2),
        cost_estimate=cost(0, 0),
        name="hidden",
    )(w_gate, w_up, w_down, *sums, *operands)


def down_kernel(targets, width, hidden_ref, down_ref, *outs):
    me = lax.axis_index("pd")
    for out, m in zip(outs, targets):
        at = pl.ds(pl.multiple_of((me ^ m) * width, width), width)
        product = jnp.dot(hidden_ref[...], down_ref[:, at], preferred_element_type=f32)
        out[...] = product.astype(out.dtype)


def down(targets, width, hidden, w_down, dtype):
    out_shape = [jax.ShapeDtypeStruct((hidden.shape[0], width), dtype)] * len(targets)
    return pl.pallas_call(
        functools.partial(down_kernel, targets, width),
        out_shape=out_shape,
        in_specs=[VMEM, VMEM],
        out_specs=[VMEM] * len(out_shape),
        compiler_params=params(out_shape * 2),
        cost_estimate=cost(2 * hidden.shape[0] * w_down.size, 2 * w_down.size),
        name="down",
    )(hidden, w_down)


def attend_kernel(order, pd_count, width, dest_ref, len_ref, query_ref, *refs):
    pieces, out_ref = refs[:-1], refs[-1]
    ep_count = len(order)
    own, me = lax.axis_index("ep"), lax.axis_index("pd")
    rows, latr = query_ref.shape
    first, second, wide = fold_widths(latr)
    part, heads = CAP // 2, rows // ep_count
    keys = []
    for ref in pieces:
        count = ref.shape[0] // CAP
        folded = ref[:, width:].astype(f32).reshape(count, CAP, wide)
        whole = jnp.concatenate([folded[:, :part, :first], folded[:, part:, :second]], axis=2)
        keys.append(whole.reshape(count * part, latr))
    keys = jnp.concatenate(keys, axis=0).astype(bf16)
    shape = (1, keys.shape[0])
    column = lax.broadcasted_iota(i32, shape, 1)
    place = column // part % ep_count
    position = (me ^ (column // (part * ep_count))) * part + column % part
    length, slot = jnp.zeros(shape, i32), jnp.zeros(shape, i32)
    for i, d in enumerate(order):
        j = own ^ d
        here = i32(0)
        for k in range(ep_count):
            here = jnp.where(dest_ref[j, k] == own, len_ref[j * ep_count + k], here)
        length = jnp.where(place == i, here, length)
        slot = jnp.where(place == i, j, slot)
    slot = jnp.where(position < length, slot, -1)
    usable = lax.broadcasted_iota(i32, (rows, 1), 0) // heads == slot
    scores = lax.dot_general(
        query_ref[...], keys, (((1,), (1,)), ((), ())), preferred_element_type=f32
    )
    scores = scores * score_scale
    top = jnp.max(jnp.where(usable, scores, -1e30), axis=1, keepdims=True)
    weights = jnp.where(usable, jnp.exp(scores - top), 0.0)
    total = jnp.sum(weights, axis=1, keepdims=True)
    summed = jnp.dot(weights.astype(bf16), keys[:, :LATC], preferred_element_type=f32)
    out_ref[...] = (summed / total).astype(bf16)


def combine_kernel(cuts, counts, table_ref, *refs):
    blocks, (out_ref, held_ref, sems) = refs[:-3], refs[-3:]
    rows, at = [], 0
    for count in counts:
        block = blocks[at][...]
        if count == 2:
            block = (block.astype(f32) + blocks[at + 1][...].astype(f32)).astype(bf16)
        rows.append(block)
        at += count
    rows = jnp.concatenate(rows * 2, axis=0)
    table, width = table_ref[...], held_ref.shape[1] // cuts
    copies = []
    for c in range(cuts):
        at = pl.ds(c * width, width)
        mixed = jnp.dot(
            table, rows[:, c * width : (c + 1) * width], preferred_element_type=f32
        )
        held_ref[:, at] = mixed.astype(bf16)
        copies.append(pltpu.make_async_copy(held_ref.at[:, at], out_ref.at[:, at], sems.at[c]))
        copies[-1].start()
    for copy in copies:
        copy.wait()


def mix(table, blocks):
    operands = [part for block in blocks for part in block]
    mixed = jax.ShapeDtypeStruct((table.shape[0], operands[0].shape[1]), bf16)
    cuts = 2 if mixed.shape[1] % 256 == 0 else 1
    return pl.pallas_call(
        functools.partial(combine_kernel, cuts, [len(block) for block in blocks]),
        out_shape=mixed,
        in_specs=[VMEM] * (1 + len(operands)),
        out_specs=HBM,
        scratch_shapes=[pltpu.VMEM(mixed.shape, bf16), pltpu.SemaphoreType.DMA((cuts,))],
        compiler_params=params([mixed] * 4 + operands * 2),
        cost_estimate=cost(4 * CAP * len(blocks) * mixed.size, 2 * mixed.size),
        name="combine",
    )(table, *operands)


def spread(pieces, m, bit):
    have = [m]
    while bit:
        for k in list(have):
            pieces[k ^ bit] = [swap(g, "pd", bit) for g in pieces[k]]
            have.append(k ^ bit)
        bit //= 2


def on_device(
    tokens,
    expert_ids,
    gate_scores,
    gate_weight,
    up_weight,
    down_weight,
    cache_rows,
    lengths,
    destination,
    decode_query,
):
    ep_count = lax.axis_size("ep")
    pd_count = lax.axis_size("pd")
    width = tokens.shape[1]
    ids = expert_ids.T

    blocks = route(ids, tokens, cache_rows, destination, ep_count)
    bit = pd_count // 2
    direct = [1]
    staged = [d for d in range(1, ep_count) if d not in direct]
    order = [0, *direct, *staged]
    arrived = [blocks[0]] + [swap(blocks[d], "ep", d) for d in range(1, ep_count)]
    over = [swap(blocks[0], "pd", bit)]
    over += [join([swap_both(blocks[d], d, bit)]) for d in direct]
    w_gate, w_up, table = fetch(
        [gate_weight[0], up_weight[0]], [], (ids, gate_scores.T), ep_count
    )
    rest = join([arrived[d] for d in staged], [table])

    pieces = {0: [join([arrived[d] for d in [0, *direct]], [rest])], bit: [join(over, [rest])]}
    pieces[bit] += [swap(tie(rest, pieces[0] + over[1:]), "pd", bit)]
    pieces[0] += [join([arrived[d] for d in staged], pieces[0])]
    (w_down,) = fetch([down_weight[0]], pieces[0])
    spread(pieces, 0, bit // 2)
    sums = gate_up([0], width, w_gate, w_up, pieces)
    pieces[bit][-1] = tie(pieces[bit][-1], [sums[0], w_down])
    spread(pieces, bit, bit // 2)
    sums = gate_up(list(range(1, bit + 1)), width, w_gate, w_up, pieces, before=sums)
    late = list(range(bit + 1, pd_count))
    others = sorted([m for m in range(pd_count) if m & 1], reverse=True)
    stay = sorted([m for m in range(pd_count) if not m & 1], reverse=True)
    hidden, part = hidden_units_of(
        late, others[0], width, w_gate, w_up, w_down, sums, pieces
    )
    parts = {others[0]: part}
    parts.update(zip(others[1:], down(others[1:], width, hidden, w_down, bf16)))
    kept = dict(zip(stay, down(stay, width, hidden, w_down, f32)))
    direct = [ep_count - 1]
    summed = [d for d in order if d and d not in direct]
    groups = [[d] for d in direct] + [[0], summed]
    shares = [(order.index(group[0]) * CAP, len(group) * CAP) for group in groups]
    for m in stay:
        kinds = [bf16 if m & bit or i < len(direct) else f32 for i in range(len(groups))]
        kept[m] = total(
            kept[m],
            swap(parts[m ^ 1], "pd", 1),
            [(at, rows, kind) for (at, rows), kind in zip(shares, kinds)],
        )
    operands = [g for m in range(pd_count) for g in pieces[m]]
    queries = decode_query.reshape(-1, decode_query.shape[3])
    attended = jax.ShapeDtypeStruct((queries.shape[0], LATC), bf16)
    attended = pl.pallas_call(
        functools.partial(attend_kernel, order, pd_count, width),
        out_shape=attended,
        in_specs=[SMEM, SMEM, VMEM] + [VMEM] * len(operands),
        out_specs=VMEM,
        compiler_params=params(operands + [queries, attended] * 4, 12 << 20),
        cost_estimate=cost(8 * CAP * ep_count * tokens.size, 8 * tokens.size),
        name="attend",
    )(*map(in_hbm, [destination, lengths, queries]), *operands)

    staged = total(
        kept[0][-1],
        swap(kept[bit][-1], "pd", bit),
        [(i * CAP, CAP, bf16) for i in range(len(summed))],
    )
    returned = {d: [swap(block, "ep", d)] for d, block in zip(summed, staged)}
    for i, d in enumerate(direct):
        returned[d] = [swap(kept[0][i], "ep", d), swap_both(kept[bit][i], d, bit)]
    returned[0] = total(kept[0][-2], swap(kept[bit][-2], "pd", bit), [(0, CAP, bf16)])
    returned = [returned[d] for d in range(ep_count)]
    mixed = mix(table, returned)
    return (mixed, attended.reshape(decode_query.shape[:3] + (LATC,)))


def solution(mesh):
    in_specs = (
        P(("group", "ep"), "pd"),
        P(("group", "ep"), None),
        P(("group", "ep"), None),
        P("ep", None, "pd"),
        P("ep", None, "pd"),
        P("ep", "pd", None),
        P(("group", "ep"), "pd", None),
        P("group"),
        P("group", None),
        P(("group", "ep"), None, "pd", None),
    )
    out_specs = (P(("group", "ep"), "pd"), P(("group", "ep"), None, "pd", None))
    return jax.shard_map(
        on_device, mesh=mesh, in_specs=in_specs, out_specs=out_specs, check_vma=False
    )
```

```python
import functools

import jax
import jax.numpy as jnp
from jax import lax
from jax.experimental import pallas as pl
from jax.experimental.pallas import tpu as pltpu
from jax.sharding import PartitionSpec as P

LATC = 512
CAP = 16

score_scale = 192.0 ** (-0.5)

bf16, f32, i32 = jnp.bfloat16, jnp.float32, jnp.int32
VMEM = pl.BlockSpec(memory_space=pltpu.VMEM)
SMEM = pl.BlockSpec(memory_space=pltpu.SMEM)
HBM = pl.BlockSpec(memory_space=pltpu.HBM)
ANY = pl.BlockSpec(memory_space=pl.ANY)


def swap(value, axis, mask):
    count = lax.axis_size(axis)
    return lax.ppermute(value, axis, [(i, i ^ mask) for i in range(count)])


def swap_both(value, ep_mask, pd_mask):
    ep_count, pd_count = lax.axis_size("ep"), lax.axis_size("pd")
    pairs = [
        (i * pd_count + j, (i ^ ep_mask) * pd_count + (j ^ pd_mask))
        for i in range(ep_count)
        for j in range(pd_count)
    ]
    return lax.ppermute(value, ("ep", "pd"), pairs)


def in_hbm(value):
    return pltpu.with_memory_space_constraint(value, pltpu.HBM)


def params(arrays, extra=6 << 20):
    held = sum(a.size * a.dtype.itemsize for a in arrays)
    return pltpu.CompilerParams(vmem_limit_bytes=min(held + extra, 60 << 20))


def cost(flops, moved=0):
    return pl.CostEstimate(flops=flops, bytes_accessed=moved, transcendentals=0)


def fold_widths(latr):
    first = latr // 2 // 128 * 128
    return first, latr - first, -(-(latr - first) // 128) * 128


def slots_of(ids, own, ep_count):
    token_count = ids.shape[1]
    served = []
    for d in range(ep_count):
        named = jnp.where(ids == (own ^ d), 1.0, 0.0)
        served.append(jnp.sum(named, axis=0, keepdims=True))
    shape = (token_count, token_count)
    earlier = lax.broadcasted_iota(i32, shape, 0) < lax.broadcasted_iota(i32, shape, 1)
    marks = jnp.concatenate(served, axis=0)
    rank = jnp.dot(
        marks.astype(bf16), jnp.where(earlier, 1.0, 0.0).astype(bf16), preferred_element_type=f32
    )
    rank = jnp.where(marks > 0.5, rank, -1.0)
    slots = lax.broadcasted_iota(i32, (CAP, token_count), 0).astype(f32)
    return [slots == rank[d : d + 1] for d in range(ep_count)]


def route_kernel(ep_count, *refs):
    sources, blocks = refs[:4], refs[4 : 4 + ep_count]
    held, sems = refs[4 + ep_count : -1], refs[-1]
    copies = [pltpu.make_async_copy(sources[i], held[i], sems.at[i]) for i in range(4)]
    for copy in copies:
        copy.start()
    ids_ref, dest_ref, cache_ref, tokens_ref = held
    own = lax.axis_index("ep")
    width = tokens_ref.shape[1]
    first, second, wide = fold_widths(cache_ref.shape[2])
    part = cache_ref.shape[1]
    copies[0].wait()
    chosen = slots_of(ids_ref[...], own, ep_count)
    dispatch = jnp.concatenate([jnp.where(c, 1.0, 0.0) for c in chosen], axis=0).astype(bf16)
    copies[1].wait()
    copies[2].wait()
    for d in range(ep_count):
        pick = i32(0)
        for k in range(ep_count):
            pick = jnp.where(dest_ref[own, k] == (own ^ d), k, pick)
        kept = cache_ref[pick].astype(f32)
        above = jnp.concatenate([kept[:, :first], jnp.zeros((part, wide - first), f32)], axis=1)
        below = jnp.concatenate([kept[:, first:], jnp.zeros((part, wide - second), f32)], axis=1)
        blocks[d][:, width:] = jnp.concatenate([above, below], axis=0).astype(bf16)
    copies[3].wait()
    rows = jnp.dot(dispatch, tokens_ref[...], preferred_element_type=f32)
    for d in range(ep_count):
        blocks[d][:, :width] = rows[d * CAP : (d + 1) * CAP].astype(bf16)


def route(ids, tokens, cache_rows, destination, ep_count):
    width = tokens.shape[1]
    wide = fold_widths(cache_rows.shape[2])[2]
    sources = [ids, destination, cache_rows, tokens]
    out_shape = [jax.ShapeDtypeStruct((CAP, width + wide), bf16)] * ep_count
    places = [pltpu.VMEM, pltpu.SMEM, pltpu.VMEM, pltpu.VMEM]
    return pl.pallas_call(
        functools.partial(route_kernel, ep_count),
        out_shape=out_shape,
        in_specs=[HBM] * 4,
        out_specs=[VMEM] * ep_count,
        scratch_shapes=[p(a.shape, a.dtype) for p, a in zip(places, sources)]
        + [pltpu.SemaphoreType.DMA((4,))],
        compiler_params=params(sources * 2 + out_shape * 2),
        cost_estimate=cost(4 * ep_count * CAP * tokens.size, 2 * tokens.size),
        name="route",
    )(*map(in_hbm, sources))


def gate_table(ids, gates, ep_count):
    own = lax.axis_index("ep")
    chosen = slots_of(ids, own, ep_count)
    table = []
    for d in range(ep_count):
        named = ids == (own ^ d)
        gate = jnp.sum(jnp.where(named, gates, 0.0), axis=0, keepdims=True)
        table.append(jnp.where(chosen[d], gate, 0.0))
    table = jnp.concatenate(table, axis=0)
    high = table.astype(bf16).astype(f32)
    return jnp.concatenate([high, table - high], axis=0).T.astype(bf16)


def fetch_kernel(ep_count, count, skip, *refs):
    routing = refs[-4:-1] if ep_count else ()
    sources, outs, sems = refs[:count], refs[skip : -1 - len(routing)], refs[-1]
    cuts, copies = sems.shape[1], []
    small = [
        pltpu.make_async_copy(refs[count + i], routing[i], routing[2].at[i])
        for i in range(2 if routing else 0)
    ]
    for copy in small:
        copy.start()
    for i in range(count):
        rows = sources[i].shape[0] // cuts
        for c in range(cuts):
            at = pl.ds(c * rows, rows)
            copies.append(
                pltpu.make_async_copy(sources[i].at[at], outs[i].at[at], sems.at[i, c])
            )
    for copy in copies:
        copy.start()
    if len(outs) > count:
        for copy in small:
            copy.wait()
        outs[-1][...] = gate_table(routing[0][...], routing[1][...], ep_count)
    for copy in copies:
        copy.wait()


def fetch(arrays, after=(), routing=(), ep_count=0):
    operands = [in_hbm(a) for a in [*arrays, *routing]]
    out_shape = [pltpu.VMEM(a.shape, a.dtype) for a in arrays]
    table, scratch = [], []
    if routing:
        scratch = [pltpu.VMEM(a.shape, a.dtype) for a in routing] + [pltpu.SemaphoreType.DMA((2,))]
        table = [jax.ShapeDtypeStruct((routing[0].shape[1], 2 * ep_count * CAP), bf16)]
    return pl.pallas_call(
        functools.partial(fetch_kernel, ep_count, len(arrays), len(operands) + len(after)),
        out_shape=out_shape + table,
        in_specs=[HBM] * len(operands) + [ANY] * len(after),
        out_specs=[VMEM] * len(out_shape + table),
        scratch_shapes=scratch + [pltpu.SemaphoreType.DMA((len(arrays), 4))],
        compiler_params=params(table * 4, 1 << 20),
        cost_estimate=cost(0, 0),
        name="fetch",
    )(*operands, *after)


def join_kernel(count, *refs):
    out_ref, at = refs[-1], 0
    for ref in refs[:count]:
        out_ref[at : at + ref.shape[0], :] = ref[...]
        at += ref.shape[0]


def join(blocks, after=(), weight=0):
    rows = sum(b.shape[0] for b in blocks)
    out_shape = jax.ShapeDtypeStruct((rows, blocks[0].shape[1]), blocks[0].dtype)
    return pl.pallas_call(
        functools.partial(join_kernel, len(blocks)),
        out_shape=out_shape,
        in_specs=[VMEM] * len(blocks) + [ANY] * len(after),
        out_specs=VMEM,
        compiler_params=params([out_shape] * 3, 1 << 20),
        cost_estimate=cost(0, weight),
        name="join",
    )(*blocks, *after)


def tie_kernel(*refs):
    pass


def tie(value, after):
    return pl.pallas_call(
        tie_kernel,
        out_shape=jax.ShapeDtypeStruct(value.shape, value.dtype),
        in_specs=[ANY] * (1 + len(after)),
        out_specs=ANY,
        input_output_aliases={0: 0},
        compiler_params=pltpu.CompilerParams(vmem_limit_bytes=1 << 20),
        cost_estimate=cost(0, 0),
        name="tie",
    )(value, *after)


def total_kernel(cuts, kept_ref, arrived_ref, *outs):
    for out, at in zip(outs, cuts):
        rows = pl.ds(at, out.shape[0])
        out[...] = (kept_ref[rows, :].astype(f32) + arrived_ref[rows, :].astype(f32)).astype(out.dtype)


def total(kept, arrived, pieces):
    out_shape = [jax.ShapeDtypeStruct((rows, kept.shape[1]), dtype) for _, rows, dtype in pieces]
    return pl.pallas_call(
        functools.partial(total_kernel, [at for at, _, _ in pieces]),
        out_shape=out_shape,
        in_specs=[VMEM, VMEM],
        out_specs=[VMEM] * len(out_shape),
        compiler_params=params([kept] * 4, 1 << 20),
        cost_estimate=cost(0, 0),
        name="total",
    )(kept, arrived)


def piece_sums(piece_refs, masks, me, width, gate_ref, up_ref):
    gate_sums = up_sums = None
    for refs, m in zip(piece_refs, masks):
        rows = jnp.concatenate([r[:, :width] for r in refs], axis=0)
        at = pl.ds(pl.multiple_of((me ^ m) * width, width), width)
        g = jnp.dot(rows, gate_ref[at, :], preferred_element_type=f32)
        u = jnp.dot(rows, up_ref[at, :], preferred_element_type=f32)
        gate_sums = g if gate_sums is None else gate_sums + g
        up_sums = u if up_sums is None else up_sums + u
    return gate_sums, up_sums


def gate_up_kernel(masks, width, has_sums, gate_ref, up_ref, *refs):
    before, refs = (refs[:2], refs[2:]) if has_sums else ((), refs)
    pieces, outs = refs[:-2], refs[-2:]
    per = len(pieces) // len(masks)
    groups = [pieces[i * per : (i + 1) * per] for i in range(len(masks))]
    sums = piece_sums(groups, masks, lax.axis_index("pd"), width, gate_ref, up_ref)
    for i in range(2):
        outs[i][...] = sums[i] + before[i][...] if has_sums else sums[i]


def gate_up(masks, width, w_gate, w_up, pieces, before=()):
    operands = [g for m in masks for g in pieces[m]]
    rows = sum(g.shape[0] for g in pieces[masks[0]])
    sums = jax.ShapeDtypeStruct((rows, w_gate.shape[1]), f32)
    return pl.pallas_call(
        functools.partial(gate_up_kernel, masks, width, bool(before)),
        out_shape=[sums, sums],
        in_specs=[VMEM] * (2 + len(before) + len(operands)),
        out_specs=[VMEM, VMEM],
        compiler_params=params(operands * 2),
        cost_estimate=cost(0, 0),
        name="gate_up",
    )(w_gate, w_up, *before, *operands)


def hidden_kernel(masks, target, width, gate_ref, up_ref, down_ref, *refs):
    (gsum_ref, usum_ref), pieces, (hidden_ref, out_ref) = refs[:2], refs[2:-2], refs[-2:]
    per = len(pieces) // len(masks)
    groups = [pieces[i * per : (i + 1) * per] for i in range(len(masks))]
    me = lax.axis_index("pd")
    gate_sums, up_sums = piece_sums(groups, masks, me, width, gate_ref, up_ref)
    gate_sums, up_sums = gate_sums + gsum_ref[...], up_sums + usum_ref[...]
    hidden = (gate_sums / (1.0 + jnp.exp(-gate_sums)) * up_sums).astype(bf16)
    hidden_ref[...] = hidden
    at = pl.ds(pl.multiple_of((me ^ target) * width, width), width)
    out_ref[...] = jnp.dot(hidden, down_ref[:, at], preferred_element_type=f32).astype(bf16)


def hidden_units_of(masks, target, width, w_gate, w_up, w_down, sums, pieces):
    operands = [g for m in masks for g in pieces[m]]
    rows, units = sums[0].shape
    out_shape = [jax.ShapeDtypeStruct((rows, n), bf16) for n in (units, width)]
    return pl.pallas_call(
        functools.partial(hidden_kernel, masks, target, width),
        out_shape=out_shape,
        in_specs=[VMEM] * (5 + len(operands)),
        out_specs=[VMEM] * 2,
        compiler_params=params(operands * 2 + out_shape * 2),
        cost_estimate=cost(0, 0),
        name="hidden",
    )(w_gate, w_up, w_down, *sums, *operands)


def down_kernel(targets, width, hidden_ref, down_ref, *outs):
    me = lax.axis_index("pd")
    for out, m in zip(outs, targets):
        at = pl.ds(pl.multiple_of((me ^ m) * width, width), width)
        product = jnp.dot(hidden_ref[...], down_ref[:, at], preferred_element_type=f32)
        out[...] = product.astype(out.dtype)


def down(targets, width, hidden, w_down, dtype):
    out_shape = [jax.ShapeDtypeStruct((hidden.shape[0], width), dtype)] * len(targets)
    return pl.pallas_call(
        functools.partial(down_kernel, targets, width),
        out_shape=out_shape,
        in_specs=[VMEM, VMEM],
        out_specs=[VMEM] * len(out_shape),
        compiler_params=params(out_shape * 2),
        cost_estimate=cost(2 * hidden.shape[0] * w_down.size, 2 * w_down.size),
        name="down",
    )(hidden, w_down)


def attend_kernel(order, pd_count, width, dest_ref, len_ref, query_ref, *refs):
    pieces, out_ref = refs[:-1], refs[-1]
    ep_count = len(order)
    own, me = lax.axis_index("ep"), lax.axis_index("pd")
    rows, latr = query_ref.shape
    first, second, wide = fold_widths(latr)
    part, heads = CAP // 2, rows // ep_count
    keys = []
    for ref in pieces:
        count = ref.shape[0] // CAP
        folded = ref[:, width:].astype(f32).reshape(count, CAP, wide)
        whole = jnp.concatenate([folded[:, :part, :first], folded[:, part:, :second]], axis=2)
        keys.append(whole.reshape(count * part, latr))
    keys = jnp.concatenate(keys, axis=0).astype(bf16)
    shape = (1, keys.shape[0])
    column = lax.broadcasted_iota(i32, shape, 1)
    place = column // part % ep_count
    position = (me ^ (column // (part * ep_count))) * part + column % part
    length, slot = jnp.zeros(shape, i32), jnp.zeros(shape, i32)
    for i, d in enumerate(order):
        j = own ^ d
        here = i32(0)
        for k in range(ep_count):
            here = jnp.where(dest_ref[j, k] == own, len_ref[j * ep_count + k], here)
        length = jnp.where(place == i, here, length)
        slot = jnp.where(place == i, j, slot)
    slot = jnp.where(position < length, slot, -1)
    usable = lax.broadcasted_iota(i32, (rows, 1), 0) // heads == slot
    scores = lax.dot_general(
        query_ref[...], keys, (((1,), (1,)), ((), ())), preferred_element_type=f32
    )
    scores = scores * score_scale
    top = jnp.max(jnp.where(usable, scores, -1e30), axis=1, keepdims=True)
    weights = jnp.where(usable, jnp.exp(scores - top), 0.0)
    total = jnp.sum(weights, axis=1, keepdims=True)
    summed = jnp.dot(weights.astype(bf16), keys[:, :LATC], preferred_element_type=f32)
    out_ref[...] = (summed / total).astype(bf16)


def combine_kernel(cuts, counts, table_ref, *refs):
    blocks, (out_ref, held_ref, sems) = refs[:-3], refs[-3:]
    rows, at = [], 0
    for count in counts:
        block = blocks[at][...]
        if count == 2:
            block = (block.astype(f32) + blocks[at + 1][...].astype(f32)).astype(bf16)
        rows.append(block)
        at += count
    rows = jnp.concatenate(rows * 2, axis=0)
    table, width = table_ref[...], held_ref.shape[1] // cuts
    copies = []
    for c in range(cuts):
        at = pl.ds(c * width, width)
        mixed = jnp.dot(
            table, rows[:, c * width : (c + 1) * width], preferred_element_type=f32
        )
        held_ref[:, at] = mixed.astype(bf16)
        copies.append(pltpu.make_async_copy(held_ref.at[:, at], out_ref.at[:, at], sems.at[c]))
        copies[-1].start()
    for copy in copies:
        copy.wait()


def mix(table, blocks):
    operands = [part for block in blocks for part in block]
    mixed = jax.ShapeDtypeStruct((table.shape[0], operands[0].shape[1]), bf16)
    cuts = 2 if mixed.shape[1] % 256 == 0 else 1
    return pl.pallas_call(
        functools.partial(combine_kernel, cuts, [len(block) for block in blocks]),
        out_shape=mixed,
        in_specs=[VMEM] * (1 + len(operands)),
        out_specs=HBM,
        scratch_shapes=[pltpu.VMEM(mixed.shape, bf16), pltpu.SemaphoreType.DMA((cuts,))],
        compiler_params=params([mixed] * 4 + operands * 2),
        cost_estimate=cost(4 * CAP * len(blocks) * mixed.size, 2 * mixed.size),
        name="combine",
    )(table, *operands)


def spread(pieces, m, bit):
    have = [m]
    while bit:
        for k in list(have):
            pieces[k ^ bit] = [swap(g, "pd", bit) for g in pieces[k]]
            have.append(k ^ bit)
        bit //= 2


def on_device(
    tokens,
    expert_ids,
    gate_scores,
    gate_weight,
    up_weight,
    down_weight,
    cache_rows,
    lengths,
    destination,
    decode_query,
):
    ep_count = lax.axis_size("ep")
    pd_count = lax.axis_size("pd")
    width = tokens.shape[1]
    ids = expert_ids.T

    blocks = route(ids, tokens, cache_rows, destination, ep_count)
    bit = pd_count // 2
    direct = [1]
    staged = [d for d in range(1, ep_count) if d not in direct]
    order = [0, *direct, *staged]
    arrived = [blocks[0]] + [swap(blocks[d], "ep", d) for d in range(1, ep_count)]
    over = [swap(blocks[0], "pd", bit)]
    over += [join([swap_both(blocks[d], d, bit)]) for d in direct]
    w_gate, w_up, table = fetch(
        [gate_weight[0], up_weight[0]], [], (ids, gate_scores.T), ep_count
    )
    rest = join([arrived[d] for d in staged], [table])

    pieces = {0: [join([arrived[d] for d in [0, *direct]], [rest])], bit: [join(over, [rest])]}
    pieces[bit] += [swap(tie(rest, pieces[0]), "pd", bit)]
    pieces[0] += [join([arrived[d] for d in staged], pieces[0])]
    (w_down,) = fetch([down_weight[0]], [*pieces[0], *over[1:]])
    spread(pieces, 0, bit // 2)
    sums = gate_up([0], width, w_gate, w_up, pieces)
    pieces[bit][-1] = tie(pieces[bit][-1], [sums[0], w_down])
    spread(pieces, bit, bit // 2)
    sums = gate_up(list(range(1, bit + 1)), width, w_gate, w_up, pieces, before=sums)
    late = list(range(bit + 1, pd_count))
    others = sorted([m for m in range(pd_count) if m & 1], reverse=True)
    stay = sorted([m for m in range(pd_count) if not m & 1], reverse=True)
    hidden, part = hidden_units_of(
        late, others[0], width, w_gate, w_up, w_down, sums, pieces
    )
    parts = {others[0]: part}
    parts.update(zip(others[1:], down(others[1:], width, hidden, w_down, bf16)))
    kept = dict(zip(stay, down(stay, width, hidden, w_down, f32)))
    direct = [ep_count - 1]
    summed = [d for d in order if d and d not in direct]
    groups = [[d] for d in direct] + [[0], summed]
    shares = [(order.index(group[0]) * CAP, len(group) * CAP) for group in groups]
    for m in stay:
        kinds = [bf16 if m & bit or i < len(direct) else f32 for i in range(len(groups))]
        kept[m] = total(
            kept[m],
            swap(parts[m ^ 1], "pd", 1),
            [(at, rows, kind) for (at, rows), kind in zip(shares, kinds)],
        )
    operands = [g for m in range(pd_count) for g in pieces[m]]
    queries = decode_query.reshape(-1, decode_query.shape[3])
    attended = jax.ShapeDtypeStruct((queries.shape[0], LATC), bf16)
    attended = pl.pallas_call(
        functools.partial(attend_kernel, order, pd_count, width),
        out_shape=attended,
        in_specs=[SMEM, SMEM, VMEM] + [VMEM] * len(operands),
        out_specs=VMEM,
        compiler_params=params(operands + [queries, attended] * 4, 12 << 20),
        cost_estimate=cost(8 * CAP * ep_count * tokens.size, 8 * tokens.size),
        name="attend",
    )(*map(in_hbm, [destination, lengths, queries]), *operands)

    staged = total(
        kept[0][-1],
        swap(kept[bit][-1], "pd", bit),
        [(i * CAP, CAP, bf16) for i in range(len(summed))],
    )
    returned = {d: [swap(block, "ep", d)] for d, block in zip(summed, staged)}
    for i, d in enumerate(direct):
        returned[d] = [swap(kept[0][i], "ep", d), swap_both(kept[bit][i], d, bit)]
    returned[0] = total(kept[0][-2], swap(kept[bit][-2], "pd", bit), [(0, CAP, bf16)])
    returned = [returned[d] for d in range(ep_count)]
    mixed = mix(table, returned)
    return (mixed, attended.reshape(decode_query.shape[:3] + (LATC,)))


def solution(mesh):
    in_specs = (
        P(("group", "ep"), "pd"),
        P(("group", "ep"), None),
        P(("group", "ep"), None),
        P("ep", None, "pd"),
        P("ep", None, "pd"),
        P("ep", "pd", None),
        P(("group", "ep"), "pd", None),
        P("group"),
        P("group", None),
        P(("group", "ep"), None, "pd", None),
    )
    out_specs = (P(("group", "ep"), "pd"), P(("group", "ep"), None, "pd", None))
    return jax.shard_map(
        on_device, mesh=mesh, in_specs=in_specs, out_specs=out_specs, check_vma=False
    )
```

```python
import functools

import jax
import jax.numpy as jnp
from jax import lax
from jax.experimental import pallas as pl
from jax.experimental.pallas import tpu as pltpu
from jax.sharding import PartitionSpec as P

LATC = 512
CAP = 16

score_scale = 192.0 ** (-0.5)

bf16, f32, i32 = jnp.bfloat16, jnp.float32, jnp.int32
VMEM = pl.BlockSpec(memory_space=pltpu.VMEM)
SMEM = pl.BlockSpec(memory_space=pltpu.SMEM)
HBM = pl.BlockSpec(memory_space=pltpu.HBM)
ANY = pl.BlockSpec(memory_space=pl.ANY)


def swap(value, axis, mask):
    count = lax.axis_size(axis)
    return lax.ppermute(value, axis, [(i, i ^ mask) for i in range(count)])


def swap_both(value, ep_mask, pd_mask):
    ep_count, pd_count = lax.axis_size("ep"), lax.axis_size("pd")
    pairs = [
        (i * pd_count + j, (i ^ ep_mask) * pd_count + (j ^ pd_mask))
        for i in range(ep_count)
        for j in range(pd_count)
    ]
    return lax.ppermute(value, ("ep", "pd"), pairs)


def in_hbm(value):
    return pltpu.with_memory_space_constraint(value, pltpu.HBM)


def params(arrays, extra=6 << 20):
    held = sum(a.size * a.dtype.itemsize for a in arrays)
    return pltpu.CompilerParams(vmem_limit_bytes=min(held + extra, 60 << 20))


def cost(flops, moved=0):
    return pl.CostEstimate(flops=flops, bytes_accessed=moved, transcendentals=0)


def fold_widths(latr):
    first = latr // 2 // 128 * 128
    return first, latr - first, -(-(latr - first) // 128) * 128


def slots_of(ids, own, ep_count):
    token_count = ids.shape[1]
    served = []
    for d in range(ep_count):
        named = jnp.where(ids == (own ^ d), 1.0, 0.0)
        served.append(jnp.sum(named, axis=0, keepdims=True))
    shape = (token_count, token_count)
    earlier = lax.broadcasted_iota(i32, shape, 0) < lax.broadcasted_iota(i32, shape, 1)
    marks = jnp.concatenate(served, axis=0)
    rank = jnp.dot(
        marks.astype(bf16), jnp.where(earlier, 1.0, 0.0).astype(bf16), preferred_element_type=f32
    )
    rank = jnp.where(marks > 0.5, rank, -1.0)
    slots = lax.broadcasted_iota(i32, (CAP, token_count), 0).astype(f32)
    return [slots == rank[d : d + 1] for d in range(ep_count)]


def route_kernel(ep_count, *refs):
    sources, blocks = refs[:4], refs[4 : 4 + ep_count]
    held, sems = refs[4 + ep_count : -1], refs[-1]
    copies = [pltpu.make_async_copy(sources[i], held[i], sems.at[i]) for i in range(3)]
    half = held[3].shape[1] // 2
    for i in range(2):
        at = pl.ds(i * half, half)
        copies.append(
            pltpu.make_async_copy(sources[3].at[:, at], held[3].at[:, at], sems.at[3 + i])
        )
    for copy in copies:
        copy.start()
    ids_ref, dest_ref, cache_ref, tokens_ref = held
    own = lax.axis_index("ep")
    width = tokens_ref.shape[1]
    first, second, wide = fold_widths(cache_ref.shape[2])
    part = cache_ref.shape[1]
    copies[0].wait()
    chosen = slots_of(ids_ref[...], own, ep_count)
    dispatch = jnp.concatenate([jnp.where(c, 1.0, 0.0) for c in chosen], axis=0).astype(bf16)
    copies[1].wait()
    copies[2].wait()
    for d in range(ep_count):
        pick = i32(0)
        for k in range(ep_count):
            pick = jnp.where(dest_ref[own, k] == (own ^ d), k, pick)
        kept = cache_ref[pick].astype(f32)
        above = jnp.concatenate([kept[:, :first], jnp.zeros((part, wide - first), f32)], axis=1)
        below = jnp.concatenate([kept[:, first:], jnp.zeros((part, wide - second), f32)], axis=1)
        blocks[d][:, width:] = jnp.concatenate([above, below], axis=0).astype(bf16)
    for i in range(2):
        at = pl.ds(i * half, half)
        copies[3 + i].wait()
        rows = jnp.dot(dispatch, tokens_ref[:, at], preferred_element_type=f32)
        for d in range(ep_count):
            blocks[d][:, at] = rows[d * CAP : (d + 1) * CAP].astype(bf16)


def route(ids, tokens, cache_rows, destination, ep_count):
    width = tokens.shape[1]
    wide = fold_widths(cache_rows.shape[2])[2]
    sources = [ids, destination, cache_rows, tokens]
    out_shape = [jax.ShapeDtypeStruct((CAP, width + wide), bf16)] * ep_count
    places = [pltpu.VMEM, pltpu.SMEM, pltpu.VMEM, pltpu.VMEM]
    return pl.pallas_call(
        functools.partial(route_kernel, ep_count),
        out_shape=out_shape,
        in_specs=[HBM] * 4,
        out_specs=[VMEM] * ep_count,
        scratch_shapes=[p(a.shape, a.dtype) for p, a in zip(places, sources)]
        + [pltpu.SemaphoreType.DMA((5,))],
        compiler_params=params(sources * 2 + out_shape * 2),
        cost_estimate=cost(4 * ep_count * CAP * tokens.size, 2 * tokens.size),
        name="route",
    )(*map(in_hbm, sources))


def gate_table(ids, gates, ep_count):
    own = lax.axis_index("ep")
    chosen = slots_of(ids, own, ep_count)
    table = []
    for d in range(ep_count):
        named = ids == (own ^ d)
        gate = jnp.sum(jnp.where(named, gates, 0.0), axis=0, keepdims=True)
        table.append(jnp.where(chosen[d], gate, 0.0))
    table = jnp.concatenate(table, axis=0)
    high = table.astype(bf16).astype(f32)
    return jnp.concatenate([high, table - high], axis=0).T.astype(bf16)


def fetch_kernel(ep_count, count, skip, *refs):
    routing = refs[-4:-1] if ep_count else ()
    sources, outs, sems = refs[:count], refs[skip : -1 - len(routing)], refs[-1]
    cuts, copies = sems.shape[1], []
    small = [
        pltpu.make_async_copy(refs[count + i], routing[i], routing[2].at[i])
        for i in range(2 if routing else 0)
    ]
    for copy in small:
        copy.start()
    for i in range(count):
        rows = sources[i].shape[0] // cuts
        for c in range(cuts):
            at = pl.ds(c * rows, rows)
            copies.append(
                pltpu.make_async_copy(sources[i].at[at], outs[i].at[at], sems.at[i, c])
            )
    for copy in copies:
        copy.start()
    if len(outs) > count:
        for copy in small:
            copy.wait()
        outs[-1][...] = gate_table(routing[0][...], routing[1][...], ep_count)
    for copy in copies:
        copy.wait()


def fetch(arrays, after=(), routing=(), ep_count=0):
    operands = [in_hbm(a) for a in [*arrays, *routing]]
    out_shape = [pltpu.VMEM(a.shape, a.dtype) for a in arrays]
    table, scratch = [], []
    if routing:
        scratch = [pltpu.VMEM(a.shape, a.dtype) for a in routing] + [pltpu.SemaphoreType.DMA((2,))]
        table = [jax.ShapeDtypeStruct((routing[0].shape[1], 2 * ep_count * CAP), bf16)]
    return pl.pallas_call(
        functools.partial(fetch_kernel, ep_count, len(arrays), len(operands) + len(after)),
        out_shape=out_shape + table,
        in_specs=[HBM] * len(operands) + [ANY] * len(after),
        out_specs=[VMEM] * len(out_shape + table),
        scratch_shapes=scratch + [pltpu.SemaphoreType.DMA((len(arrays), 4))],
        compiler_params=params(table * 4, 1 << 20),
        cost_estimate=cost(0, 0),
        name="fetch",
    )(*operands, *after)


def join_kernel(count, *refs):
    out_ref, at = refs[-1], 0
    for ref in refs[:count]:
        out_ref[at : at + ref.shape[0], :] = ref[...]
        at += ref.shape[0]


def join(blocks, after=(), weight=0):
    rows = sum(b.shape[0] for b in blocks)
    out_shape = jax.ShapeDtypeStruct((rows, blocks[0].shape[1]), blocks[0].dtype)
    return pl.pallas_call(
        functools.partial(join_kernel, len(blocks)),
        out_shape=out_shape,
        in_specs=[VMEM] * len(blocks) + [ANY] * len(after),
        out_specs=VMEM,
        compiler_params=params([out_shape] * 3, 1 << 20),
        cost_estimate=cost(0, weight),
        name="join",
    )(*blocks, *after)


def tie_kernel(*refs):
    pass


def tie(value, after):
    return pl.pallas_call(
        tie_kernel,
        out_shape=jax.ShapeDtypeStruct(value.shape, value.dtype),
        in_specs=[ANY] * (1 + len(after)),
        out_specs=ANY,
        input_output_aliases={0: 0},
        compiler_params=pltpu.CompilerParams(vmem_limit_bytes=1 << 20),
        cost_estimate=cost(0, 0),
        name="tie",
    )(value, *after)


def total_kernel(cuts, kept_ref, arrived_ref, *outs):
    for out, at in zip(outs, cuts):
        rows = pl.ds(at, out.shape[0])
        out[...] = (kept_ref[rows, :].astype(f32) + arrived_ref[rows, :].astype(f32)).astype(out.dtype)


def total(kept, arrived, pieces):
    out_shape = [jax.ShapeDtypeStruct((rows, kept.shape[1]), dtype) for _, rows, dtype in pieces]
    return pl.pallas_call(
        functools.partial(total_kernel, [at for at, _, _ in pieces]),
        out_shape=out_shape,
        in_specs=[VMEM, VMEM],
        out_specs=[VMEM] * len(out_shape),
        compiler_params=params([kept] * 4, 1 << 20),
        cost_estimate=cost(0, 0),
        name="total",
    )(kept, arrived)


def piece_sums(piece_refs, masks, me, width, gate_ref, up_ref):
    gate_sums = up_sums = None
    for refs, m in zip(piece_refs, masks):
        rows = jnp.concatenate([r[:, :width] for r in refs], axis=0)
        at = pl.ds(pl.multiple_of((me ^ m) * width, width), width)
        g = jnp.dot(rows, gate_ref[at, :], preferred_element_type=f32)
        u = jnp.dot(rows, up_ref[at, :], preferred_element_type=f32)
        gate_sums = g if gate_sums is None else gate_sums + g
        up_sums = u if up_sums is None else up_sums + u
    return gate_sums, up_sums


def gate_up_kernel(masks, width, has_sums, gate_ref, up_ref, *refs):
    before, refs = (refs[:2], refs[2:]) if has_sums else ((), refs)
    pieces, outs = refs[:-2], refs[-2:]
    per = len(pieces) // len(masks)
    groups = [pieces[i * per : (i + 1) * per] for i in range(len(masks))]
    sums = piece_sums(groups, masks, lax.axis_index("pd"), width, gate_ref, up_ref)
    for i in range(2):
        outs[i][...] = sums[i] + before[i][...] if has_sums else sums[i]


def gate_up(masks, width, w_gate, w_up, pieces, before=()):
    operands = [g for m in masks for g in pieces[m]]
    rows = sum(g.shape[0] for g in pieces[masks[0]])
    sums = jax.ShapeDtypeStruct((rows, w_gate.shape[1]), f32)
    return pl.pallas_call(
        functools.partial(gate_up_kernel, masks, width, bool(before)),
        out_shape=[sums, sums],
        in_specs=[VMEM] * (2 + len(before) + len(operands)),
        out_specs=[VMEM, VMEM],
        compiler_params=params(operands * 2),
        cost_estimate=cost(0, 0),
        name="gate_up",
    )(w_gate, w_up, *before, *operands)


def hidden_kernel(masks, target, width, gate_ref, up_ref, down_ref, *refs):
    (gsum_ref, usum_ref), pieces, (hidden_ref, out_ref) = refs[:2], refs[2:-2], refs[-2:]
    per = len(pieces) // len(masks)
    groups = [pieces[i * per : (i + 1) * per] for i in range(len(masks))]
    me = lax.axis_index("pd")
    gate_sums, up_sums = piece_sums(groups, masks, me, width, gate_ref, up_ref)
    gate_sums, up_sums = gate_sums + gsum_ref[...], up_sums + usum_ref[...]
    hidden = (gate_sums / (1.0 + jnp.exp(-gate_sums)) * up_sums).astype(bf16)
    hidden_ref[...] = hidden
    at = pl.ds(pl.multiple_of((me ^ target) * width, width), width)
    out_ref[...] = jnp.dot(hidden, down_ref[:, at], preferred_element_type=f32).astype(bf16)


def hidden_units_of(masks, target, width, w_gate, w_up, w_down, sums, pieces):
    operands = [g for m in masks for g in pieces[m]]
    rows, units = sums[0].shape
    out_shape = [jax.ShapeDtypeStruct((rows, n), bf16) for n in (units, width)]
    return pl.pallas_call(
        functools.partial(hidden_kernel, masks, target, width),
        out_shape=out_shape,
        in_specs=[VMEM] * (5 + len(operands)),
        out_specs=[VMEM] * 2,
        compiler_params=params(operands * 2 + out_shape * 2),
        cost_estimate=cost(0, 0),
        name="hidden",
    )(w_gate, w_up, w_down, *sums, *operands)


def down_kernel(targets, width, hidden_ref, down_ref, *outs):
    me = lax.axis_index("pd")
    for out, m in zip(outs, targets):
        at = pl.ds(pl.multiple_of((me ^ m) * width, width), width)
        product = jnp.dot(hidden_ref[...], down_ref[:, at], preferred_element_type=f32)
        out[...] = product.astype(out.dtype)


def down(targets, width, hidden, w_down, dtype):
    out_shape = [jax.ShapeDtypeStruct((hidden.shape[0], width), dtype)] * len(targets)
    return pl.pallas_call(
        functools.partial(down_kernel, targets, width),
        out_shape=out_shape,
        in_specs=[VMEM, VMEM],
        out_specs=[VMEM] * len(out_shape),
        compiler_params=params(out_shape * 2),
        cost_estimate=cost(2 * hidden.shape[0] * w_down.size, 2 * w_down.size),
        name="down",
    )(hidden, w_down)


def attend_kernel(order, pd_count, width, dest_ref, len_ref, query_ref, *refs):
    pieces, out_ref = refs[:-1], refs[-1]
    ep_count = len(order)
    own, me = lax.axis_index("ep"), lax.axis_index("pd")
    rows, latr = query_ref.shape
    first, second, wide = fold_widths(latr)
    part, heads = CAP // 2, rows // ep_count
    keys = []
    for ref in pieces:
        count = ref.shape[0] // CAP
        folded = ref[:, width:].astype(f32).reshape(count, CAP, wide)
        whole = jnp.concatenate([folded[:, :part, :first], folded[:, part:, :second]], axis=2)
        keys.append(whole.reshape(count * part, latr))
    keys = jnp.concatenate(keys, axis=0).astype(bf16)
    shape = (1, keys.shape[0])
    column = lax.broadcasted_iota(i32, shape, 1)
    place = column // part % ep_count
    position = (me ^ (column // (part * ep_count))) * part + column % part
    length, slot = jnp.zeros(shape, i32), jnp.zeros(shape, i32)
    for i, d in enumerate(order):
        j = own ^ d
        here = i32(0)
        for k in range(ep_count):
            here = jnp.where(dest_ref[j, k] == own, len_ref[j * ep_count + k], here)
        length = jnp.where(place == i, here, length)
        slot = jnp.where(place == i, j, slot)
    slot = jnp.where(position < length, slot, -1)
    usable = lax.broadcasted_iota(i32, (rows, 1), 0) // heads == slot
    scores = lax.dot_general(
        query_ref[...], keys, (((1,), (1,)), ((), ())), preferred_element_type=f32
    )
    scores = scores * score_scale
    top = jnp.max(jnp.where(usable, scores, -1e30), axis=1, keepdims=True)
    weights = jnp.where(usable, jnp.exp(scores - top), 0.0)
    total = jnp.sum(weights, axis=1, keepdims=True)
    summed = jnp.dot(weights.astype(bf16), keys[:, :LATC], preferred_element_type=f32)
    out_ref[...] = (summed / total).astype(bf16)


def combine_kernel(cuts, counts, table_ref, *refs):
    blocks, (out_ref, held_ref, sems) = refs[:-3], refs[-3:]
    rows, at = [], 0
    for count in counts:
        block = blocks[at][...]
        if count == 2:
            block = (block.astype(f32) + blocks[at + 1][...].astype(f32)).astype(bf16)
        rows.append(block)
        at += count
    rows = jnp.concatenate(rows * 2, axis=0)
    table, width = table_ref[...], held_ref.shape[1] // cuts
    copies = []
    for c in range(cuts):
        at = pl.ds(c * width, width)
        mixed = jnp.dot(
            table, rows[:, c * width : (c + 1) * width], preferred_element_type=f32
        )
        held_ref[:, at] = mixed.astype(bf16)
        copies.append(pltpu.make_async_copy(held_ref.at[:, at], out_ref.at[:, at], sems.at[c]))
        copies[-1].start()
    for copy in copies:
        copy.wait()


def mix(table, blocks):
    operands = [part for block in blocks for part in block]
    mixed = jax.ShapeDtypeStruct((table.shape[0], operands[0].shape[1]), bf16)
    cuts = 7 if mixed.shape[1] % 896 == 0 else 1
    return pl.pallas_call(
        functools.partial(combine_kernel, cuts, [len(block) for block in blocks]),
        out_shape=mixed,
        in_specs=[VMEM] * (1 + len(operands)),
        out_specs=HBM,
        scratch_shapes=[pltpu.VMEM(mixed.shape, bf16), pltpu.SemaphoreType.DMA((cuts,))],
        compiler_params=params([mixed] * 4 + operands * 2),
        cost_estimate=cost(4 * CAP * len(blocks) * mixed.size, 2 * mixed.size),
        name="combine",
    )(table, *operands)


def spread(pieces, m, bit):
    have = [m]
    while bit:
        for k in list(have):
            pieces[k ^ bit] = [swap(g, "pd", bit) for g in pieces[k]]
            have.append(k ^ bit)
        bit //= 2


def on_device(
    tokens,
    expert_ids,
    gate_scores,
    gate_weight,
    up_weight,
    down_weight,
    cache_rows,
    lengths,
    destination,
    decode_query,
):
    ep_count = lax.axis_size("ep")
    pd_count = lax.axis_size("pd")
    width = tokens.shape[1]
    ids = expert_ids.T

    blocks = route(ids, tokens, cache_rows, destination, ep_count)
    bit = pd_count // 2
    direct = [1]
    staged = [d for d in range(1, ep_count) if d not in direct]
    order = [0, *direct, *staged]
    arrived = [blocks[0]] + [swap(blocks[d], "ep", d) for d in range(1, ep_count)]
    over = [swap(blocks[0], "pd", bit)]
    over += [join([swap_both(blocks[d], d, bit)]) for d in direct]
    w_gate, w_up, table = fetch(
        [gate_weight[0], up_weight[0]], [], (ids, gate_scores.T), ep_count
    )
    rest = join([arrived[d] for d in staged], [table])

    pieces = {0: [join([arrived[d] for d in [0, *direct]], [rest])], bit: [join(over, [rest])]}
    pieces[bit] += [swap(tie(rest, pieces[0]), "pd", bit)]
    pieces[0] += [join([arrived[d] for d in staged], pieces[0])]
    (w_down,) = fetch([down_weight[0]], [*pieces[0], *over[1:]])
    spread(pieces, 0, bit // 2)
    sums = gate_up([0], width, w_gate, w_up, pieces)
    pieces[bit][-1] = tie(pieces[bit][-1], [sums[0], w_down])
    spread(pieces, bit, bit // 2)
    sums = gate_up(list(range(1, bit + 1)), width, w_gate, w_up, pieces, before=sums)
    late = list(range(bit + 1, pd_count))
    others = sorted([m for m in range(pd_count) if m & 1], reverse=True)
    stay = sorted([m for m in range(pd_count) if not m & 1], reverse=True)
    hidden, part = hidden_units_of(
        late, others[0], width, w_gate, w_up, w_down, sums, pieces
    )
    parts = {others[0]: part}
    parts.update(zip(others[1:], down(others[1:], width, hidden, w_down, bf16)))
    kept = dict(zip(stay, down(stay, width, hidden, w_down, f32)))
    direct = [ep_count - 1]
    summed = [d for d in order if d and d not in direct]
    groups = [[d] for d in direct] + [[0], summed]
    shares = [(order.index(group[0]) * CAP, len(group) * CAP) for group in groups]
    for m in stay:
        kinds = [bf16 if m & bit or i < len(direct) else f32 for i in range(len(groups))]
        kept[m] = total(
            kept[m],
            swap(parts[m ^ 1], "pd", 1),
            [(at, rows, kind) for (at, rows), kind in zip(shares, kinds)],
        )
    operands = [g for m in range(pd_count) for g in pieces[m]]
    queries = decode_query.reshape(-1, decode_query.shape[3])
    attended = jax.ShapeDtypeStruct((queries.shape[0], LATC), bf16)
    attended = pl.pallas_call(
        functools.partial(attend_kernel, order, pd_count, width),
        out_shape=attended,
        in_specs=[SMEM, SMEM, VMEM] + [VMEM] * len(operands),
        out_specs=VMEM,
        compiler_params=params(operands + [queries, attended] * 4, 12 << 20),
        cost_estimate=cost(8 * CAP * ep_count * tokens.size, 8 * tokens.size),
        name="attend",
    )(*map(in_hbm, [destination, lengths, queries]), *operands)

    staged = total(
        kept[0][-1],
        swap(kept[bit][-1], "pd", bit),
        [(i * CAP, CAP, bf16) for i in range(len(summed))],
    )
    returned = {d: [swap(block, "ep", d)] for d, block in zip(summed, staged)}
    for i, d in enumerate(direct):
        returned[d] = [swap(kept[0][i], "ep", d), swap_both(kept[bit][i], d, bit)]
    returned[0] = total(kept[0][-2], swap(kept[bit][-2], "pd", bit), [(0, CAP, bf16)])
    returned = [returned[d] for d in range(ep_count)]
    mixed = mix(table, returned)
    return (mixed, attended.reshape(decode_query.shape[:3] + (LATC,)))


def solution(mesh):
    in_specs = (
        P(("group", "ep"), "pd"),
        P(("group", "ep"), None),
        P(("group", "ep"), None),
        P("ep", None, "pd"),
        P("ep", None, "pd"),
        P("ep", "pd", None),
        P(("group", "ep"), "pd", None),
        P("group"),
        P("group", None),
        P(("group", "ep"), None, "pd", None),
    )
    out_specs = (P(("group", "ep"), "pd"), P(("group", "ep"), None, "pd", None))
    return jax.shard_map(
        on_device, mesh=mesh, in_specs=in_specs, out_specs=out_specs, check_vma=False
    )
```
